32 devices in a mesh: chan: 4 (over z), bl: 4 (over y, x), pol: 2 (over core).
Axes of the slice: x: 2, y: 2, z: 4, core: 2. Of those that a mesh axis runs over, the one named last changes fastest.
Arguments:
- visibilities: bfloat16 [2, 20480, 2, 256], P('pol', ('chan', 'bl')), may hold values from -1.5 to 1.5
- uv_coords: bfloat16 [20480, 2, 256], P(('chan', 'bl')), may hold values from -12 to 12
- block_slot: int32 [20480], P('chan'), may hold values from 0 to 63, as said below
- slot_table: int32 [3, 256], P(None, ('chan', 'bl')), may hold values from 0 to 2016, as said below
Outputs:
- stokes_grid: float32 [2, 2, 2048, 2048], P('pol', None, 'bl', 'chan')
The draws below stay inside these ranges and needn't reach their ends.
Inputs may be any that keep to these rules, and one draw needn't show every extreme that they name: `block_slot`: entry j names a subgrid of block j's channel group; that subgrid's owner is entry // 16. Within the 1280 blocks of one baseline shard in one channel group (aligned runs of 1280 entries) no owner is named more than 640 times, and in every channel group one owner is named exactly 640 times by every shard. `slot_table`: column g belongs to subgrid g mod (64) of channel group g // 64, owned by shard b = (g // 16) mod 4. Row 0 is its corner's grid row, from b * 512 to (b + 1) * 512 - 32; row 1 its corner's grid column, up to 2016; row 2 its w-plane, below 32.
All inputs are finite; a program needn't handle non-finite values.
Results may differ from the reference program's by a relative error of at most 0.0035.
Values may be sent and summed in bfloat16 or wider, within the bound.
No kernel may reach another device: no remote copies, remote signals or barrier semaphores. Data moves between devices by JAX's collectives and lax.ppermute only.
A program may use at most 64 MiB of HBM per device.

```python
import math
import jax
import jax.numpy as jnp
from jax import lax

G = 2048
SUB = 32
VB = 256
WPLANES = 32
NB_DEV = 1280
SLOTS = 16
GROUPS = 4
SHARDS = 4
POLS = 2
NBLK = 20480


def draw_block_slot(key, part):
    key = jax.random.fold_in(key, 11)
    key_hot, key_rest, key_slot, key_order = jax.random.split(key, 4)
    capacity = NB_DEV // 2
    hot_owner = jax.random.randint(key_hot, (GROUPS, 1, 1), 0, SHARDS)
    shifts = jax.random.randint(key_rest, (GROUPS, SHARDS, NB_DEV), 1, SHARDS)
    positions = jnp.arange(NB_DEV, dtype=jnp.int32)[None, None, :]
    owners = jnp.where(positions < capacity, hot_owner, (hot_owner + shifts) % SHARDS)
    scores = jax.random.randint(key_order, (GROUPS, SHARDS, NB_DEV), 0, 2 ** 30 // NB_DEV) * NB_DEV + positions
    ordering = jnp.argsort(scores, axis=2, stable=True)
    owners = jnp.take_along_axis(owners, ordering, axis=2)
    local_slot = jax.random.randint(key_slot, (GROUPS, SHARDS, NB_DEV), 0, SLOTS)
    return (owners * SLOTS + local_slot).reshape(GROUPS * SHARDS * NB_DEV).astype(jnp.int32)


def draw_slot_table(key, part):
    key = jax.random.fold_in(key, 23)
    subkeys = jax.random.split(key, 6)
    total_slots = GROUPS * SHARDS * SLOTS
    strip_rows = G // SHARDS
    positions = jnp.arange(total_slots, dtype=jnp.int32)
    owners = positions // SLOTS % SHARDS
    local_row = jax.random.randint(subkeys[0], (total_slots,), 0, strip_rows - SUB + 1)
    column = jax.random.randint(subkeys[1], (total_slots,), 0, G - SUB + 1)
    planes = jax.random.randint(subkeys[2], (total_slots,), 0, WPLANES)
    lowest = jax.random.randint(subkeys[3], (), 0, total_slots)
    highest_slot = (jax.random.randint(subkeys[4], (), 0, GROUPS) * SHARDS + SHARDS - 1) * SLOTS + jax.random.randint(subkeys[5], (), 0, SLOTS)
    local_row = jnp.where(positions == lowest, 0, local_row)
    column = jnp.where(positions == lowest, 0, column)
    local_row = jnp.where(positions == highest_slot, strip_rows - SUB, local_row)
    column = jnp.where(positions == highest_slot, G - SUB, column)
    return jnp.stack([owners * strip_rows + local_row, column, planes]).astype(jnp.int32)


def shard_levels(key, dims, cuts, low, high):
    gain = 1.0
    for position, parts in cuts:
        heights = jax.random.uniform(jax.random.fold_in(jax.random.fold_in(key, 6), position), (parts,), jnp.float32, low / len(cuts), high / len(cuts))
        gain = gain * jnp.repeat(jnp.exp(heights), dims[position] // parts).reshape((-1,) + (1,) * (len(dims) - 1 - position))
    return gain


def normal_values(key, extent, deviation, reach, pieces=(), kind=jnp.bfloat16):
    values = jax.random.normal(key, extent, jnp.float32) * deviation
    if len(pieces) > 0:
        values = shard_levels(key, extent, pieces, -0.22, 0.18) * values
    return jnp.clip(values, min=-reach, max=reach).astype(kind)


def setup_inputs(seed: int = 0) -> dict:
    keys = jax.random.split(jax.random.key(seed), 5)
    return {
        "visibilities": normal_values(keys[0], (POLS, NBLK, 2, VB), 0.25, 1.5, ((0, 2), (1, 16))),
        "uv_coords": jnp.clip(jax.random.uniform(keys[1], (NBLK, 2, VB), jnp.float32, -12.0, 12.0) * shard_levels(keys[1], (NBLK, 2, VB), ((0, 16),), -0.4, 0.0), -12.0, 12.0).astype(jnp.bfloat16),
        "block_slot": draw_block_slot(jax.random.fold_in(keys[4], 71), 0),
        "slot_table": draw_slot_table(jax.random.fold_in(keys[4], 71), 0),
    }


two_pi = 2.0 * math.pi
w_step = 0.25
highest = lax.Precision.HIGHEST

def pixel_offsets():
    return (jnp.arange(SUB, dtype=jnp.float32) - SUB // 2) / SUB

def kernel_images(packed):
    offsets = pixel_offsets()
    norm_scale = 1.0 / math.sqrt(VB)
    u_pos = packed[:, 2, :].astype(jnp.float32)
    v_pos = packed[:, 3, :].astype(jnp.float32)
    vis_real = packed[:, 0, :].astype(jnp.float32)[:, None, :]
    vis_imag = packed[:, 1, :].astype(jnp.float32)[:, None, :]
    angle_u = two_pi * u_pos[:, None, :] * offsets[None, :, None]
    left_phasor = jnp.concatenate([jnp.cos(angle_u), jnp.sin(angle_u)], axis=1).astype(jnp.bfloat16)
    angle_v = two_pi * v_pos[:, None, :] * offsets[None, :, None]
    phase_real = jnp.cos(angle_v) * norm_scale
    phase_imag = jnp.sin(angle_v) * norm_scale
    weighted_real = vis_real * phase_real - vis_imag * phase_imag
    weighted_imag = vis_real * phase_imag + vis_imag * phase_real
    right_phasor = jnp.concatenate([weighted_real, weighted_imag], axis=1).astype(jnp.bfloat16)
    left_phasor = lax.optimization_barrier(left_phasor)
    right_phasor = lax.optimization_barrier(right_phasor)
    product = jnp.einsum('kav,kbv->kab', left_phasor.astype(jnp.float32), right_phasor.astype(jnp.float32), precision=highest)
    real_part = product[:, :SUB, :SUB] - product[:, SUB:, SUB:]
    imag_part = product[:, :SUB, SUB:] + product[:, SUB:, :SUB]
    return jnp.stack([real_part, imag_part], axis=1).reshape(packed.shape[0], 2 * SUB * SUB)

def subgrid_transform(images, planes):
    slot_count = images.shape[0]
    cells = images.reshape(slot_count, 2, SUB, SUB)
    real_part = cells[:, 0]
    imag_part = cells[:, 1]
    offsets = pixel_offsets()
    tapers = jnp.sin(math.pi * (jnp.arange(SUB, dtype=jnp.float32) + 0.5) / SUB)
    taper_grid = tapers[:, None] * tapers[None, :]
    n_term = jnp.sqrt(1.0 - offsets[:, None] ** 2 - offsets[None, :] ** 2) - 1.0
    w_phase = (0.0 - two_pi * w_step) * planes.astype(jnp.float32)[:, None, None] * n_term[None, :, :]
    screen_cos = jnp.cos(w_phase)
    screen_sin = jnp.sin(w_phase)
    tapered_real = taper_grid * (real_part * screen_cos - imag_part * screen_sin)
    tapered_imag = taper_grid * (real_part * screen_sin + imag_part * screen_cos)
    centred = jnp.arange(SUB, dtype=jnp.int32) - SUB // 2
    product_mod = centred[:, None] * centred[None, :] % SUB
    angles = (0.0 - two_pi) * product_mod.astype(jnp.float32) / SUB
    dft_real = jnp.cos(angles) / math.sqrt(SUB)
    dft_imag = jnp.sin(angles) / math.sqrt(SUB)

    def along_rows(matrix, values):
        return jnp.einsum('kl,slm->skm', matrix, values, precision=highest)

    def along_cols(values, matrix):
        return jnp.einsum('skm,jm->skj', values, matrix, precision=highest)
    rows_real = along_rows(dft_real, tapered_real) - along_rows(dft_imag, tapered_imag)
    rows_imag = along_rows(dft_real, tapered_imag) + along_rows(dft_imag, tapered_real)
    cols_real = along_cols(rows_real, dft_real) - along_cols(rows_imag, dft_imag)
    cols_imag = along_cols(rows_real, dft_imag) + along_cols(rows_imag, dft_real)
    return jnp.stack([cols_real, cols_imag], axis=1)

def place_dense(subgrids, row_corner, col_corner, strip_rows, grid_cols):
    empty_strip = jnp.zeros((2, strip_rows, grid_cols), jnp.float32)
    zero_index = jnp.zeros((), jnp.int32)

    def add_one(which, current):
        row_at = row_corner[which].astype(jnp.int32)
        col_at = col_corner[which].astype(jnp.int32)
        window = lax.dynamic_slice(current, (zero_index, row_at, col_at), (2, SUB, SUB))
        return lax.dynamic_update_slice(current, window + subgrids[which], (zero_index, row_at, col_at))
    return lax.fori_loop(0, subgrids.shape[0], add_one, empty_strip)

def reference(visibilities, uv_coords, block_slot, slot_table):
    total_slots = GROUPS * SHARDS * SLOTS
    total_blocks = GROUPS * SHARDS * NB_DEV
    group_size = 128 if total_blocks % 128 == 0 else NB_DEV
    group_count = total_blocks // group_size
    group_of = jnp.arange(total_blocks, dtype=jnp.int32) // (SHARDS * NB_DEV)
    global_slot = (group_of * (SHARDS * SLOTS) + block_slot).astype(jnp.int32)
    coords_groups = uv_coords.reshape(group_count, group_size, 2, VB)
    slot_groups = global_slot.reshape(group_count, group_size)
    grids = []
    for polarization in range(POLS):
        vis_groups = visibilities[polarization].reshape(group_count, group_size, 2, VB)

        def add_group(totals, inputs):
            vis_part, coord_part, slot_part = inputs
            packed = jnp.concatenate([vis_part, coord_part], axis=1)
            return (totals.at[slot_part].add(kernel_images(packed)), None)
        totals, _ = lax.scan(add_group, jnp.zeros((total_slots, 2 * SUB * SUB), jnp.float32), (vis_groups, coords_groups, slot_groups))
        subgrids = subgrid_transform(totals, slot_table[2])
        grids.append(place_dense(subgrids, slot_table[0], slot_table[1], G, G))
    return jnp.stack([0.5 * (grids[0] + grids[1]), 0.5 * (grids[0] - grids[1])])
```

```python
import functools
import math

import jax
import jax.numpy as jnp
import numpy as np
from jax import lax
from jax.experimental import pallas as pl
from jax.experimental.pallas import tpu as pltpu
from jax.sharding import PartitionSpec as P

G = 2048
SUB = 32
VB = 256
HALF = SUB // 2
LANES = 128
ROWS = 40
W_STEP = 0.25
highest = lax.Precision.HIGHEST
f32 = jnp.float32
bf16 = jnp.bfloat16


def cos_sin(angle, terms):
    square = angle * angle
    cos_sum = f32((-1.0) ** (terms - 1) / math.factorial(2 * terms - 2))
    sin_sum = f32((-1.0) ** (terms - 1) / math.factorial(2 * terms - 1))
    for n in range(terms - 2, -1, -1):
        cos_sum = cos_sum * square + f32((-1.0) ** n / math.factorial(2 * n))
        sin_sum = sin_sum * square + f32((-1.0) ** n / math.factorial(2 * n + 1))
    return cos_sum, sin_sum * angle


def multiples(coords):
    c_half, s_half = cos_sin(coords * (math.pi / SUB), 6)
    cosines = {1: 1.0 - 2.0 * s_half * s_half}
    sines = {1: 2.0 * s_half * c_half}
    for k in range(2, HALF + 1):
        base = 1 << ((k - 1).bit_length() - 1)
        twice = 2.0 * cosines[base]
        if k == 2 * base:
            cosines[k] = twice * cosines[base] - 1.0
            sines[k] = twice * sines[base]
        else:
            cosines[k] = twice * cosines[k - base] - cosines[2 * base - k]
            sines[k] = twice * sines[k - base] + sines[2 * base - k]
    return cosines, sines


GROUP = 8
BATCH = 2


def phases(start, scale, inputs, angles, values, coords):
    first, uv_ref, mine_ref, theirs_ref = inputs
    for group in range(BATCH):
        block = start + group * GROUP
        there = pl.ds(pl.multiple_of(block * 4, 4 * GROUP), 4 * GROUP)
        here = pl.ds(pl.multiple_of(first + block * 4, 4 * GROUP), 4 * GROUP)
        coords[...] = uv_ref[here, :].astype(f32)
        for part in range(2):
            for side in range(2):
                at = (group * 2 + part) * 8 * SUB
                cosines, sines = multiples(coords[pl.ds(part * 16 + side, 8, 2), :])
                for k in range(1, HALF + 1):
                    angles[side, at + (k - 1) * 8 : at + k * 8, :] = cosines[k]
                    angles[side, at + (HALF + k - 1) * 8 : at + (HALF + k) * 8, :] = sines[k]
        rows = slice(group * 4 * GROUP, (group + 1) * 4 * GROUP)
        values[0, rows, :] = mine_ref[here, :].astype(f32) * scale
        values[1, rows, :] = theirs_ref[there, :].astype(f32) * scale


def operands(angles, values, left, right):
    last = lax.broadcasted_iota(jnp.int32, (HALF, LANES), 0) == HALF - 1
    for block in range(BATCH * GROUP):
        for half in range(2):
            chunk = 2 * block + half
            lanes = slice(half * LANES, (half + 1) * LANES)
            at = pl.ds(chunk // 8 * 8 * SUB + chunk % 8, SUB, 8)
            left[block, :SUB, lanes] = angles[0, at, :].astype(bf16)
            phase = angles[1, at, :]
            cosine, sine = phase[:HALF], phase[HALF:]
            row = 0
            for product in range(2):
                real = values[product, 2 * chunk : 2 * chunk + 1, :]
                imag = values[product, 2 * chunk + 1 : 2 * chunk + 2, :]
                rc, is_, rs, ic = real * cosine, imag * sine, real * sine, imag * cosine
                for up, down, centre in ((rc - is_, rc + is_, real), (ic + rs, ic - rs, imag)):
                    right[block, row : row + HALF, lanes] = jnp.where(last, centre, up).astype(bf16)
                    right[block, row + HALF : row + SUB, lanes] = down.astype(bf16)
                    row += SUB


def products(id_at, ids_ref, left, right, sums):
    for block in range(BATCH * GROUP):
        image = lax.dot_general(
            left[block], right[block], (((1,), (1,)), ((), ())), preferred_element_type=f32
        )
        at = pl.ds(pl.multiple_of(ids_ref[id_at + block] * ROWS, 8), ROWS)
        sums[at, :] += image[:ROWS]


def slot_sums_kernel(place_ref, sign_ref, ids_ref, uv_ref, mine_ref, theirs_ref, keep_ref, send_ref, sums, *scratch):
    blocks = theirs_ref.shape[0] // 4
    step = BATCH * GROUP
    first = place_ref[0]
    id_at = place_ref[1]
    scale = 0.5 / math.sqrt(VB)
    inputs = (first * 4, uv_ref, mine_ref, theirs_ref)
    even, odd = scratch[:5], scratch[5:]
    sums[...] = jnp.zeros_like(sums)
    for left in (even[2], odd[2]):
        left[...] = jnp.ones_like(left)

    def fill(start, buffers):
        angles, values, left, right, coords = buffers
        phases(start, scale, inputs, angles, values, coords)
        operands(angles, values, left, right)

    fill(0, even)

    def two_batches(trip, carry):
        start = trip * 2 * step
        products(id_at + start, ids_ref, even[2], even[3], sums)
        fill(start + step, odd)
        products(id_at + start + step, ids_ref, odd[2], odd[3], sums)
        fill(jnp.minimum(start + 2 * step, blocks - step), even)
        return carry

    lax.fori_loop(0, blocks // (2 * step), two_batches, 0)

    owners = keep_ref.shape[0]
    pairs = sums.shape[0] // ROWS // owners // 2
    sign = sign_ref[0]
    low = lax.broadcasted_iota(jnp.int32, (1, LANES), 1) < LANES // 2

    def store(owner, rows, one, two):
        one_back, two_back = pltpu.roll(one, LANES // 2, 1), pltpu.roll(two, LANES // 2, 1)
        own = jnp.where(low, one_back + sign * one, two + sign * two_back)
        other = jnp.where(low, one - sign * one_back, two_back - sign * two)
        keep_ref[owner, rows, :] = own.astype(keep_ref.dtype)
        send_ref[owner, rows, :] = other.astype(send_ref.dtype)

    def store_owner(owner, carry):
        base = owner * (2 * pairs * ROWS)

        def rows_of(slot, row, count):
            return sums[pl.ds(pl.multiple_of(base + slot * ROWS + row, 8), count), :]

        for pair in range(pairs):
            store(
                owner, slice(pair * SUB, (pair + 1) * SUB), rows_of(pair, 0, SUB), rows_of(pairs + pair, 0, SUB)
            )
        blank = [jnp.zeros((16 - pairs, LANES), f32)]
        one = jnp.concatenate([rows_of(pair, SUB, 8)[:1] for pair in range(pairs)] + blank, axis=0)
        two = jnp.concatenate([rows_of(pairs + pair, SUB, 8)[:1] for pair in range(pairs)] + blank, axis=0)
        store(owner, slice(pairs * SUB, pairs * SUB + 16), one, two)
        return carry

    lax.fori_loop(0, owners, store_owner, 0)


def slot_sums(place, sign, block_slot, uv, mine, theirs, shard_count, slots):
    pairs = slots // 2
    rows = pairs * SUB + 16
    vmem = pl.BlockSpec(memory_space=pltpu.VMEM)
    smem = pl.BlockSpec(memory_space=pltpu.SMEM)
    buffers = [
        pltpu.VMEM((2, BATCH * 2 * GROUP * SUB, LANES), f32),
        pltpu.VMEM((2, BATCH * 4 * GROUP, LANES), f32),
        pltpu.VMEM((BATCH * GROUP, SUB + HALF, VB), bf16),
        pltpu.VMEM((BATCH * GROUP, 4 * SUB, VB), bf16),
        pltpu.VMEM((4 * GROUP, LANES), f32),
    ]
    return pl.pallas_call(
        slot_sums_kernel,
        out_shape=[
            jax.ShapeDtypeStruct((shard_count, rows, LANES), f32),
            jax.ShapeDtypeStruct((shard_count, rows, LANES), bf16),
        ],
        in_specs=[smem, smem, smem, vmem, vmem, vmem],
        out_specs=[vmem, vmem],
        scratch_shapes=[pltpu.VMEM((shard_count * slots * ROWS, LANES), f32)] + buffers + buffers,
        compiler_params=pltpu.CompilerParams(vmem_limit_bytes=32 * 1024 * 1024),
        cost_estimate=pl.CostEstimate(flops=60_000_000_000, bytes_accessed=4_000_000, transcendentals=0),
        name="slot_sums",
    )(place, sign, block_slot, uv, mine, theirs)


def row_order():
    return np.array(list(range(HALF + 1, SUB)) + [HALF] + list(range(HALF - 1, -1, -1)))


def dft_matrix():
    centred = np.arange(SUB) - HALF
    product_mod = centred[:, None] * centred[None, :] % SUB
    return np.exp(-2j * np.pi * product_mod / SUB) / math.sqrt(SUB)


def spread(matrix):
    parts = []
    for factor in (1, 1j):
        scaled = matrix * factor
        one = np.concatenate([scaled.real, scaled.imag], axis=1)
        parts.append(np.kron(np.eye(2), one))
    return np.concatenate(parts, axis=1).astype(np.float32)


def constants():
    order = row_order()
    dft = dft_matrix()
    cols = dft.T[order]
    columns = spread(np.concatenate([cols, 1j * cols], axis=0))
    rows = dft[:, order]
    rows = np.concatenate([rows.real, rows.imag], axis=1).astype(np.float32)
    offsets = (order - HALF) / SUB
    taper = np.sin(np.pi * (order + 0.5) / SUB)
    n_term = np.sqrt(1.0 - offsets[:, None] ** 2 - offsets[None, :] ** 2) - 1.0
    turns = np.tile(-W_STEP * n_term, (1, 4)).astype(np.float32)
    tapers = np.tile(taper[:, None] * taper[None, :], (1, 4)).astype(np.float32)
    return turns, tapers, columns, rows


def transform_kernel(planes_ref, sums_ref, turns_ref, tapers_ref, columns_ref, rows_ref, out_ref):
    pairs = out_ref.shape[0]
    plain = sums_ref[0].astype(f32)
    for source in range(1, sums_ref.shape[0]):
        plain = plain + sums_ref[source].astype(f32)
    lane = lax.broadcasted_iota(jnp.int32, (1, LANES), 1)
    turned = jnp.where(
        (lane // SUB) % 2 == 0, -pltpu.roll(plain, LANES - SUB, 1), pltpu.roll(plain, SUB, 1)
    )
    last = lax.broadcasted_iota(jnp.int32, (HALF, LANES), 0) == HALF - 1
    pieces = []
    for pair in range(pairs):
        at = pair * SUB
        cos_p, sin_p = plain[at : at + HALF], plain[at + HALF : at + SUB]
        cos_t, sin_t = turned[at : at + HALF], turned[at + HALF : at + SUB]
        zero = pairs * SUB + pair
        up = jnp.where(last, plain[zero : zero + 1], cos_p + sin_t)
        up_i = jnp.where(last, turned[zero : zero + 1], cos_t - sin_p)
        image = jnp.concatenate([up, cos_p - sin_t], axis=0)
        image_i = jnp.concatenate([up_i, cos_t + sin_p], axis=0)
        plane = jnp.where(lane < LANES // 2, planes_ref[pair], planes_ref[pairs + pair]).astype(f32)
        turns = plane * turns_ref[...]
        c_half, s_half = cos_sin((turns - jnp.floor(turns + 0.5)) * math.pi, 7)
        screen_cos = (1.0 - 2.0 * s_half * s_half) * tapers_ref[...]
        screen_sin = (2.0 * s_half * c_half) * tapers_ref[...]
        pieces.append(image * screen_cos + image_i * screen_sin)
    both = jnp.dot(jnp.concatenate(pieces, axis=0), columns_ref[...], precision=highest, preferred_element_type=f32)
    for pair in range(pairs):
        at = slice(pair * SUB, (pair + 1) * SUB)
        stacked = jnp.concatenate([both[at, :LANES], both[at, LANES:]], axis=0)
        out_ref[pair] = jnp.dot(rows_ref[...], stacked, precision=highest, preferred_element_type=f32).astype(
            out_ref.dtype
        )


def subgrid_transform(sums, planes, slots):
    vmem = pl.BlockSpec(memory_space=pltpu.VMEM)
    smem = pl.BlockSpec(memory_space=pltpu.SMEM)
    return pl.pallas_call(
        transform_kernel,
        out_shape=jax.ShapeDtypeStruct((slots // 2, SUB, LANES), bf16),
        in_specs=[smem] + [vmem] * 5,
        out_specs=vmem,
        compiler_params=pltpu.CompilerParams(vmem_limit_bytes=32 * 1024 * 1024),
        name="subgrid_transform",
    )(planes, sums, *constants())


def place_kernel(origin_ref, *refs):
    count = (len(refs) - 3) // 2
    corner_refs, sub_refs = refs[:count], refs[count : 2 * count]
    out_ref, strip, sem = refs[2 * count :]
    pairs = sub_refs[0].shape[0]
    cols = out_ref.shape[2]
    strip[...] = jnp.zeros_like(strip)
    lane = lax.broadcasted_iota(jnp.int32, (SUB, LANES), 1)

    for corner_ref, sub_ref in zip(corner_refs, sub_refs):

        def add_pair(pair, carry):
            for half in range(2):
                row = corner_ref[0, half * pairs + pair] - origin_ref[0]
                col = corner_ref[1, half * pairs + pair] - origin_ref[1]

                @pl.when((col > -SUB) & (col < cols))
                def _():
                    padded = col + LANES
                    tile = padded // LANES
                    at = padded % LANES
                    piece = sub_ref[pair].astype(f32)
                    left = (lane >= at) & (lane < at + SUB)
                    right = lane < at + SUB - LANES
                    for part in range(2):
                        start = half * 2 * SUB + part * SUB
                        turned = pltpu.roll(piece, (at + (LANES - start)) % LANES, 1)
                        rows = pl.ds(row, SUB)
                        strip[part, tile, rows, :] += jnp.where(left, turned, 0.0)
                        strip[part, tile + 1, rows, :] += jnp.where(right, turned, 0.0)

            return carry

        lax.fori_loop(0, pairs, add_pair, 0)
    copies = [
        pltpu.make_async_copy(
            strip.at[part, tile + 1], out_ref.at[part, :, pl.ds(tile * LANES, LANES)], sem.at[part, tile]
        )
        for part in range(2)
        for tile in range(cols // LANES)
    ]
    for copy in copies:
        copy.start()
    for copy in copies:
        copy.wait()


def place(origin, corners, subs, strip_rows, cols):
    smem = pl.BlockSpec(memory_space=pltpu.SMEM)
    vmem = pl.BlockSpec(memory_space=pltpu.VMEM)
    return pl.pallas_call(
        place_kernel,
        out_shape=jax.ShapeDtypeStruct((2, strip_rows, cols), f32),
        in_specs=[smem] * (1 + len(corners)) + [vmem] * len(subs),
        out_specs=pl.BlockSpec(memory_space=pl.ANY),
        scratch_shapes=[
            pltpu.VMEM((2, cols // LANES + 2, strip_rows, LANES), f32),
            pltpu.SemaphoreType.DMA((2, cols // LANES)),
        ],
        compiler_params=pltpu.CompilerParams(vmem_limit_bytes=32 * 1024 * 1024),
        name="place",
    )(origin, *corners, *subs)


def around(block, axis):
    count = lax.axis_size(axis)
    return [block] + [
        lax.ppermute(block, axis, [(i, (i + step) % count) for i in range(count)]) for step in range(1, count)
    ]


def on_device(visibilities, uv_coords, block_slot, slot_table):
    shard_count = lax.axis_size("bl")
    chan_count = lax.axis_size("chan")
    my_shard = lax.axis_index("bl")
    my_chan = lax.axis_index("chan")
    my_pol = lax.axis_index("pol")
    blocks = uv_coords.shape[0]
    slots = slot_table.shape[1]
    half = blocks // 2
    strip_rows = G // shard_count
    cols = G // chan_count

    def rows_of(values):
        count = values.shape[0]
        return values.reshape(count, 2, VB // LANES, LANES).transpose(0, 2, 1, 3).reshape(count * 4, LANES)

    vis = rows_of(visibilities[0])
    theirs = lax.ppermute(
        lax.dynamic_slice_in_dim(vis, (1 - my_pol) * (half * 4), half * 4, 0), "pol", [(0, 1), (1, 0)]
    )
    corners = around(slot_table[:2], "chan")
    sign = (1.0 - 2.0 * my_pol.astype(f32))[None]
    at = jnp.stack([my_pol * half, my_shard * blocks + my_pol * half])
    keep, send = slot_sums(at, sign, block_slot, rows_of(uv_coords), vis, theirs, shard_count, slots)
    got = lax.ppermute(send, "pol", [(0, 1), (1, 0)])
    partial = (keep + got.astype(f32)).astype(bf16)
    partial = lax.all_to_all(partial, "bl", split_axis=0, concat_axis=0, tiled=True)
    subs = around(subgrid_transform(partial, slot_table[2], slots), "chan")
    origin = jnp.stack([my_shard * strip_rows, my_chan * cols])
    return place(origin, corners, subs, strip_rows, cols)[None]


def solution(mesh):
    return jax.shard_map(
        on_device,
        mesh=mesh,
        in_specs=(
            P("pol", ("chan", "bl"), None, None),
            P(("chan", "bl"), None, None),
            P("chan"),
            P(None, ("chan", "bl")),
        ),
        out_specs=P("pol", None, "bl", "chan"),
        check_vma=False,
    )
```

```python
import functools
import math

import jax
import jax.numpy as jnp
import numpy as np
from jax import lax
from jax.experimental import pallas as pl
from jax.experimental.pallas import tpu as pltpu
from jax.sharding import PartitionSpec as P

G = 2048
SUB = 32
VB = 256
HALF = SUB // 2
LANES = 128
ROWS = 40
W_STEP = 0.25
highest = lax.Precision.HIGHEST
f32 = jnp.float32
bf16 = jnp.bfloat16


def cos_sin(angle, terms):
    square = angle * angle
    cos_sum = f32((-1.0) ** (terms - 1) / math.factorial(2 * terms - 2))
    sin_sum = f32((-1.0) ** (terms - 1) / math.factorial(2 * terms - 1))
    for n in range(terms - 2, -1, -1):
        cos_sum = cos_sum * square + f32((-1.0) ** n / math.factorial(2 * n))
        sin_sum = sin_sum * square + f32((-1.0) ** n / math.factorial(2 * n + 1))
    return cos_sum, sin_sum * angle


def multiples(coords):
    c_half, s_half = cos_sin(coords * (math.pi / SUB), 6)
    cosines = {1: 1.0 - 2.0 * s_half * s_half}
    sines = {1: 2.0 * s_half * c_half}
    for k in range(2, HALF + 1):
        base = 1 << ((k - 1).bit_length() - 1)
        twice = 2.0 * cosines[base]
        if k == 2 * base:
            cosines[k] = twice * cosines[base] - 1.0
            sines[k] = twice * sines[base]
        else:
            cosines[k] = twice * cosines[k - base] - cosines[2 * base - k]
            sines[k] = twice * sines[k - base] + sines[2 * base - k]
    return cosines, sines


GROUP = 8
BATCH = 4
PITCH = 9


def phases(start, scale, inputs, angles, values, coords):
    uv_ref, mine_ref, theirs_ref = inputs
    for group in range(BATCH):
        block = start + group * GROUP
        here = pl.ds(pl.multiple_of(block * 4, 4 * GROUP), 4 * GROUP)
        coords[...] = uv_ref[here, :].astype(f32)
        for part in range(2):
            for side in range(2):
                at = (group * 2 + part) * PITCH * SUB
                cosines, sines = multiples(coords[pl.ds(part * 16 + side, 8, 2), :])
                for k in range(1, HALF + 1):
                    row = at + (k - 1) * PITCH
                    angles[side, row : row + 8, :] = cosines[k]
                    row += HALF * PITCH
                    angles[side, row : row + 8, :] = sines[k]
        rows = slice(group * 4 * GROUP, (group + 1) * 4 * GROUP)
        values[0, rows, :] = mine_ref[here, :].astype(f32) * scale
        values[1, rows, :] = theirs_ref[here, :].astype(f32) * scale


def add_products(id_at, ids_ref, angles, values, sums):
    last = lax.broadcasted_iota(jnp.int32, (HALF, LANES), 0) == HALF - 1
    ones = jnp.ones((HALF, VB), bf16)
    for block in range(BATCH * GROUP):
        lefts, rights = [], []
        for chunk in (2 * block, 2 * block + 1):
            at = pl.ds(chunk // 8 * PITCH * SUB + chunk % 8, SUB, PITCH)
            lefts.append(angles[0, at, :].astype(bf16))
            phase = angles[1, at, :]
            cosine, sine = phase[:HALF], phase[HALF:]
            pieces = []
            for product in range(2):
                real = values[product, 2 * chunk : 2 * chunk + 1, :]
                imag = values[product, 2 * chunk + 1 : 2 * chunk + 2, :]
                rc, is_, rs, ic = real * cosine, imag * sine, real * sine, imag * cosine
                for up, down, centre in ((rc - is_, rc + is_, real), (ic + rs, ic - rs, imag)):
                    pieces.append(jnp.where(last, centre, up).astype(bf16))
                    pieces.append(down.astype(bf16))
            rights.append(jnp.concatenate(pieces, axis=0))
        image = lax.dot_general(
            jnp.concatenate([jnp.concatenate(lefts, axis=1), ones], axis=0),
            jnp.concatenate(rights, axis=1),
            (((1,), (1,)), ((), ())),
            preferred_element_type=f32,
        )
        at = pl.ds(pl.multiple_of(ids_ref[id_at + block] * ROWS, 8), ROWS)
        sums[at, :] += image[:ROWS]


def slot_sums_kernel(place_ref, sign_ref, ids_ref, uv_ref, mine_ref, theirs_ref, keep_ref, send_ref, sums, *scratch):
    local, sem, scratch = scratch[:3], scratch[3], scratch[4:]
    blocks = local[0].shape[0] // 4
    step = BATCH * GROUP
    id_at = place_ref[1]
    scale = 0.5 / math.sqrt(VB)
    own_half = pl.ds(pl.multiple_of(place_ref[0] * 4, 16), blocks * 4)
    sources = (uv_ref.at[own_half, :], mine_ref.at[own_half, :], theirs_ref)
    copies = [pltpu.make_async_copy(source, local[n], sem.at[n]) for n, source in enumerate(sources)]
    for copy in copies:
        copy.start()
    even, odd = scratch[:3], scratch[3:]
    sums[...] = jnp.zeros_like(sums)
    for copy in copies:
        copy.wait()

    def fill(start, buffers):
        phases(start, scale, local, *buffers)

    def add(start, buffers):
        add_products(id_at + start, ids_ref, buffers[0], buffers[1], sums)

    fill(0, even)

    def two_batches(trip, carry):
        start = trip * 2 * step
        add(start, even)
        fill(start + step, odd)
        add(start + step, odd)
        fill(start + 2 * step, even)
        return carry

    trips = blocks // (2 * step) - 1
    lax.fori_loop(0, trips, two_batches, 0)
    add(trips * 2 * step, even)
    fill((trips * 2 + 1) * step, odd)
    add((trips * 2 + 1) * step, odd)

    owners = keep_ref.shape[0]
    pairs = sums.shape[0] // ROWS // owners // 2
    sign = sign_ref[0]
    low = lax.broadcasted_iota(jnp.int32, (1, LANES), 1) < LANES // 2

    def store(owner, rows, one, two):
        one_back, two_back = pltpu.roll(one, LANES // 2, 1), pltpu.roll(two, LANES // 2, 1)
        own = jnp.where(low, one_back + sign * one, two + sign * two_back)
        other = jnp.where(low, one - sign * one_back, two_back - sign * two)
        keep_ref[owner, rows, :] = own.astype(keep_ref.dtype)
        send_ref[owner, rows, :] = other.astype(send_ref.dtype)

    def store_owner(owner, carry):
        base = owner * (2 * pairs * ROWS)

        def rows_of(slot, row, count):
            return sums[pl.ds(pl.multiple_of(base + slot * ROWS + row, 8), count), :]

        for pair in range(pairs):
            store(
                owner, slice(pair * SUB, (pair + 1) * SUB), rows_of(pair, 0, SUB), rows_of(pairs + pair, 0, SUB)
            )
        blank = [jnp.zeros((16 - pairs, LANES), f32)]
        one = jnp.concatenate([rows_of(pair, SUB, 8)[:1] for pair in range(pairs)] + blank, axis=0)
        two = jnp.concatenate([rows_of(pairs + pair, SUB, 8)[:1] for pair in range(pairs)] + blank, axis=0)
        store(owner, slice(pairs * SUB, pairs * SUB + 16), one, two)
        return carry

    lax.fori_loop(0, owners, store_owner, 0)


def slot_sums(place, sign, block_slot, uv, mine, theirs, shard_count, slots):
    pairs = slots // 2
    rows = pairs * SUB + 16
    vmem = pl.BlockSpec(memory_space=pltpu.VMEM)
    smem = pl.BlockSpec(memory_space=pltpu.SMEM)
    hbm = pl.BlockSpec(memory_space=pltpu.HBM)
    buffers = [
        pltpu.VMEM((2, BATCH * 2 * PITCH * SUB, LANES), f32),
        pltpu.VMEM((2, BATCH * 4 * GROUP, LANES), f32),
        pltpu.VMEM((4 * GROUP, LANES), f32),
    ]
    return pl.pallas_call(
        slot_sums_kernel,
        out_shape=[
            jax.ShapeDtypeStruct((shard_count, rows, LANES), f32),
            jax.ShapeDtypeStruct((shard_count, rows, LANES), bf16),
        ],
        in_specs=[smem, smem, smem, hbm, hbm, pl.BlockSpec(memory_space=pl.ANY)],
        out_specs=[vmem, vmem],
        scratch_shapes=[pltpu.VMEM((shard_count * slots * ROWS, LANES), f32)]
        + [pltpu.VMEM(theirs.shape, bf16)] * 3
        + [pltpu.SemaphoreType.DMA((3,))]
        + buffers
        + buffers,
        compiler_params=pltpu.CompilerParams(vmem_limit_bytes=32 * 1024 * 1024),
        cost_estimate=pl.CostEstimate(flops=60_000_000_000, bytes_accessed=4_000_000, transcendentals=0),
        name="slot_sums",
    )(place, sign, block_slot, uv, mine, theirs)


def row_order():
    return np.array(list(range(HALF + 1, SUB)) + [HALF] + list(range(HALF - 1, -1, -1)))


def dft_matrix():
    centred = np.arange(SUB) - HALF
    product_mod = centred[:, None] * centred[None, :] % SUB
    return np.exp(-2j * np.pi * product_mod / SUB) / math.sqrt(SUB)


def spread(matrix):
    parts = []
    for factor in (1, 1j):
        scaled = matrix * factor
        one = np.concatenate([scaled.real, scaled.imag], axis=1)
        parts.append(np.kron(np.eye(2), one))
    return np.concatenate(parts, axis=1).astype(np.float32)


def constants():
    order = row_order()
    dft = dft_matrix()
    cols = dft.T[order]
    columns = spread(np.concatenate([cols, 1j * cols], axis=0))
    rows = dft[:, order]
    rows = np.concatenate([rows.real, rows.imag], axis=1).astype(np.float32)
    offsets = (order - HALF) / SUB
    taper = np.sin(np.pi * (order + 0.5) / SUB)
    n_term = np.sqrt(1.0 - offsets[:, None] ** 2 - offsets[None, :] ** 2) - 1.0
    turns = np.tile(-W_STEP * n_term, (1, 4)).astype(np.float32)
    tapers = np.tile(taper[:, None] * taper[None, :], (1, 4)).astype(np.float32)
    return turns, tapers, columns, rows


def transform_kernel(planes_ref, corners_ref, sums_ref, turns_ref, tapers_ref, columns_ref, rows_ref, out_ref):
    pairs = out_ref.shape[0] // SUB
    plain = sums_ref[0].astype(f32)
    for source in range(1, sums_ref.shape[0]):
        plain = plain + sums_ref[source].astype(f32)
    lane = lax.broadcasted_iota(jnp.int32, (1, LANES), 1)
    turned = jnp.where(
        (lane // SUB) % 2 == 0, -pltpu.roll(plain, LANES - SUB, 1), pltpu.roll(plain, SUB, 1)
    )
    last = lax.broadcasted_iota(jnp.int32, (HALF, LANES), 0) == HALF - 1
    pieces = []
    for pair in range(pairs):
        at = pair * SUB
        cos_p, sin_p = plain[at : at + HALF], plain[at + HALF : at + SUB]
        cos_t, sin_t = turned[at : at + HALF], turned[at + HALF : at + SUB]
        zero = pairs * SUB + pair
        up = jnp.where(last, plain[zero : zero + 1], cos_p + sin_t)
        up_i = jnp.where(last, turned[zero : zero + 1], cos_t - sin_p)
        image = jnp.concatenate([up, cos_p - sin_t], axis=0)
        image_i = jnp.concatenate([up_i, cos_t + sin_p], axis=0)
        plane = jnp.where(lane < LANES // 2, planes_ref[pair], planes_ref[pairs + pair]).astype(f32)
        turns = plane * turns_ref[...]
        c_half, s_half = cos_sin((turns - jnp.floor(turns + 0.5)) * math.pi, 7)
        screen_cos = (1.0 - 2.0 * s_half * s_half) * tapers_ref[...]
        screen_sin = (2.0 * s_half * c_half) * tapers_ref[...]
        pieces.append(image * screen_cos + image_i * screen_sin)
    both = jnp.dot(jnp.concatenate(pieces, axis=0), columns_ref[...], precision=highest, preferred_element_type=f32)
    for pair in range(pairs):
        at = slice(pair * SUB, (pair + 1) * SUB)
        stacked = jnp.concatenate([both[at, :LANES], both[at, LANES:]], axis=0)
        out_ref[at, :] = jnp.dot(rows_ref[...], stacked, precision=highest, preferred_element_type=f32).astype(
            out_ref.dtype
        )
    out_ref[pairs * SUB :, :] = corners_ref[...].astype(out_ref.dtype)


def corner_rows(corners):
    digits = jnp.stack([corners // 16, corners % 16], axis=1).reshape(1, -1).astype(f32)
    return jnp.pad(digits, ((0, 15), (0, LANES - digits.shape[1])))


def subgrid_transform(sums, planes, corners, slots):
    vmem = pl.BlockSpec(memory_space=pltpu.VMEM)
    smem = pl.BlockSpec(memory_space=pltpu.SMEM)
    return pl.pallas_call(
        transform_kernel,
        out_shape=jax.ShapeDtypeStruct((slots // 2 * SUB + 16, LANES), bf16),
        in_specs=[smem] + [vmem] * 6,
        out_specs=vmem,
        compiler_params=pltpu.CompilerParams(vmem_limit_bytes=32 * 1024 * 1024),
        name="subgrid_transform",
    )(planes, corner_rows(corners), sums, *constants())


def place_kernel(origin_ref, *refs):
    sub_refs = refs[:-5]
    out_ref, strip, decoded, corners, sem = refs[-5:]
    pairs = sub_refs[0].shape[0] // SUB
    slots = 2 * pairs
    cols = out_ref.shape[2]
    for source, sub_ref in enumerate(sub_refs):
        digits = sub_ref[pairs * SUB :, :].astype(f32)
        joined = 16.0 * digits + pltpu.roll(digits, LANES - slots, 1)
        decoded[source * 8 : source * 8 + 8, :] = joined[:8].astype(jnp.int32)
    fetch = pltpu.make_async_copy(decoded, corners, sem.at[0, 0])
    fetch.start()
    strip[...] = jnp.zeros_like(strip)
    lane = lax.broadcasted_iota(jnp.int32, (SUB, LANES), 1)
    fetch.wait()

    for source, sub_ref in enumerate(sub_refs):

        def add_pair(pair, carry, source=source, sub_ref=sub_ref):
            for half in range(2):
                row = corners[source * 8, half * pairs + pair] - origin_ref[0]
                col = corners[source * 8, 2 * slots + half * pairs + pair] - origin_ref[1]

                @pl.when((col > -SUB) & (col < cols))
                def _():
                    padded = col + LANES
                    tile = padded // LANES
                    at = padded % LANES
                    piece = sub_ref[pl.ds(pl.multiple_of(pair * SUB, SUB), SUB), :].astype(f32)
                    left = (lane >= at) & (lane < at + SUB)
                    right = lane < at + SUB - LANES
                    for part in range(2):
                        start = half * 2 * SUB + part * SUB
                        turned = pltpu.roll(piece, (at + (LANES - start)) % LANES, 1)
                        rows = pl.ds(row, SUB)
                        strip[part, tile, rows, :] += jnp.where(left, turned, 0.0)
                        strip[part, tile + 1, rows, :] += jnp.where(right, turned, 0.0)

            return carry

        lax.fori_loop(0, pairs, add_pair, 0)
    copies = [
        pltpu.make_async_copy(
            strip.at[part, tile + 1], out_ref.at[part, :, pl.ds(tile * LANES, LANES)], sem.at[part, tile]
        )
        for part in range(2)
        for tile in range(cols // LANES)
    ]
    for copy in copies:
        copy.start()
    for copy in copies:
        copy.wait()


def place(origin, subs, strip_rows, cols):
    smem = pl.BlockSpec(memory_space=pltpu.SMEM)
    vmem = pl.BlockSpec(memory_space=pltpu.VMEM)
    return pl.pallas_call(
        place_kernel,
        out_shape=jax.ShapeDtypeStruct((2, strip_rows, cols), f32),
        in_specs=[smem] + [vmem] * len(subs),
        out_specs=pl.BlockSpec(memory_space=pl.ANY),
        scratch_shapes=[
            pltpu.VMEM((2, cols // LANES + 2, strip_rows, LANES), f32),
            pltpu.VMEM((8 * len(subs), LANES), jnp.int32),
            pltpu.SMEM((8 * len(subs), LANES), jnp.int32),
            pltpu.SemaphoreType.DMA((2, cols // LANES)),
        ],
        compiler_params=pltpu.CompilerParams(vmem_limit_bytes=32 * 1024 * 1024),
        name="place",
    )(origin, *subs)


def around(block, axis):
    count = lax.axis_size(axis)
    return [block] + [
        lax.ppermute(block, axis, [(i, (i + step) % count) for i in range(count)]) for step in range(1, count)
    ]


def on_device(visibilities, uv_coords, block_slot, slot_table):
    shard_count = lax.axis_size("bl")
    chan_count = lax.axis_size("chan")
    my_shard = lax.axis_index("bl")
    my_chan = lax.axis_index("chan")
    my_pol = lax.axis_index("pol")
    blocks = uv_coords.shape[0]
    slots = slot_table.shape[1]
    half = blocks // 2
    strip_rows = G // shard_count
    cols = G // chan_count

    def rows_of(values):
        count = values.shape[0]
        return values.reshape(count, 2, VB // LANES, LANES).transpose(0, 2, 1, 3).reshape(count * 4, LANES)

    vis = rows_of(visibilities[0])
    theirs = lax.ppermute(
        lax.dynamic_slice_in_dim(vis, (1 - my_pol) * (half * 4), half * 4, 0), "pol", [(0, 1), (1, 0)]
    )
    sign = (1.0 - 2.0 * my_pol.astype(f32))[None]
    at = jnp.stack([my_pol * half, my_shard * blocks + my_pol * half])
    keep, send = slot_sums(at, sign, block_slot, rows_of(uv_coords), vis, theirs, shard_count, slots)
    got = lax.ppermute(send, "pol", [(0, 1), (1, 0)])
    partial = (keep + got.astype(f32)).astype(bf16)
    partial = lax.all_to_all(partial, "bl", split_axis=0, concat_axis=0, tiled=True)
    subs = around(subgrid_transform(partial, slot_table[2], slot_table[:2], slots), "chan")
    origin = jnp.stack([my_shard * strip_rows, my_chan * cols])
    return place(origin, subs, strip_rows, cols)[None]


def solution(mesh):
    return jax.shard_map(
        on_device,
        mesh=mesh,
        in_specs=(
            P("pol", ("chan", "bl"), None, None),
            P(("chan", "bl"), None, None),
            P("chan"),
            P(None, ("chan", "bl")),
        ),
        out_specs=P("pol", None, "bl", "chan"),
        check_vma=False,
    )
```

```python
import functools
import math

import jax
import jax.numpy as jnp
import numpy as np
from jax import lax
from jax.experimental import pallas as pl
from jax.experimental.pallas import tpu as pltpu
from jax.sharding import PartitionSpec as P

G = 2048
SUB = 32
VB = 256
HALF = SUB // 2
LANES = 128
ROWS = 40
W_STEP = 0.25
f32 = jnp.float32
bf16 = jnp.bfloat16


def cos_sin(angle, terms):
    square = angle * angle
    cos_sum = f32((-1.0) ** (terms - 1) / math.factorial(2 * terms - 2))
    sin_sum = f32((-1.0) ** (terms - 1) / math.factorial(2 * terms - 1))
    for n in range(terms - 2, -1, -1):
        cos_sum = cos_sum * square + f32((-1.0) ** n / math.factorial(2 * n))
        sin_sum = sin_sum * square + f32((-1.0) ** n / math.factorial(2 * n + 1))
    return cos_sum, sin_sum * angle


def multiples(coords):
    c_half, s_half = cos_sin(coords * (math.pi / SUB), 6)
    cosines = {1: 1.0 - 2.0 * s_half * s_half}
    sines = {1: 2.0 * s_half * c_half}
    for k in range(2, HALF + 1):
        base = 1 << ((k - 1).bit_length() - 1)
        twice = 2.0 * cosines[base]
        if k == 2 * base:
            cosines[k] = twice * cosines[base] - 1.0
            sines[k] = twice * sines[base]
        else:
            cosines[k] = twice * cosines[k - base] - cosines[2 * base - k]
            sines[k] = twice * sines[k - base] + sines[2 * base - k]
    return cosines, sines


def odd_halves(coords):
    c_half, s_half = cos_sin(coords * (math.pi / SUB), 6)
    twice = {1: 2.0 - 4.0 * s_half * s_half}
    for base in (2, 4, 8):
        twice[base] = twice[base // 2] * twice[base // 2] - 2.0
    cosines, sines = [c_half], [s_half]
    for j in range(1, HALF):
        base = 1 << (j.bit_length() - 1)
        cosines.append(twice[base] * cosines[j - base] - cosines[2 * base - 1 - j])
        sines.append(twice[base] * sines[j - base] + sines[2 * base - 1 - j])
    return cosines, sines


GROUP = 8
BATCH = 4
PITCH = 9


def phases(start, scale, inputs, angles, values, wide):
    for group in range(BATCH):
        rows = pl.ds(pl.multiple_of((start + group * GROUP) * 4, 4 * GROUP), 4 * GROUP)
        for which, ref in enumerate(inputs):
            wide[which, : 4 * GROUP, :] = ref[rows, :].astype(f32)
        for part in range(2):
            at = (group * 2 + part) * PITCH * SUB

            def pick(which, component):
                return wide[which, pl.ds(part * 16 + component, 8, 2), :]

            def put(side, number, value):
                angles[side, at + number * PITCH : at + number * PITCH + 8, :] = value

            cosines, sines = multiples(pick(0, 0))
            for k in range(1, HALF + 1):
                put(0, k - 1, cosines[k])
                put(0, HALF + k - 1, sines[k])
            cosines, sines = odd_halves(pick(0, 1))
            for k in range(HALF):
                put(1, k, cosines[k])
                put(1, HALF + k, sines[k])
            c_half, s_half = cosines[0] * scale, sines[0] * scale
            chunks = slice((group * 2 + part) * 8, (group * 2 + part + 1) * 8)
            for product in range(2):
                real, imag = pick(1 + product, 0), pick(1 + product, 1)
                values[2 * product, chunks, :] = real * c_half + imag * s_half
                values[2 * product + 1, chunks, :] = imag * c_half - real * s_half


def add_products(id_at, ids_ref, angles, values, sums):
    ones = jnp.ones((HALF, VB), bf16)
    for block in range(BATCH * GROUP):
        lefts, rights = [], []
        for chunk in (2 * block, 2 * block + 1):
            at = pl.ds(chunk // 8 * PITCH * SUB + chunk % 8, SUB, PITCH)
            lefts.append(angles[0, at, :].astype(bf16))
            phase = angles[1, at, :]
            cosine, sine = phase[:HALF], phase[HALF:]
            pieces = []
            for product in range(2):
                real = values[2 * product, chunk : chunk + 1, :]
                imag = values[2 * product + 1, chunk : chunk + 1, :]
                rc, is_, rs, ic = real * cosine, imag * sine, real * sine, imag * cosine
                for piece in (rc - is_, rc + is_, ic + rs, ic - rs):
                    pieces.append(piece.astype(bf16))
            rights.append(jnp.concatenate(pieces, axis=0))
        image = lax.dot_general(
            jnp.concatenate([jnp.concatenate(lefts, axis=1), ones], axis=0),
            jnp.concatenate(rights, axis=1),
            (((1,), (1,)), ((), ())),
            preferred_element_type=f32,
        )
        at = pl.ds(pl.multiple_of(ids_ref[id_at + block] * ROWS, 8), ROWS)
        sums[at, :] += image[:ROWS]


def slot_sums_kernel(first_ref, sign_ref, ids_ref, uv_ref, mine_ref, theirs_ref, keep_ref, send_ref, sums, *scratch):
    local = (uv_ref, mine_ref, theirs_ref)
    blocks = uv_ref.shape[0] // 4
    step = BATCH * GROUP
    id_at = first_ref[0]
    scale = 0.5 / math.sqrt(VB)
    even, odd = scratch[:3], scratch[3:]
    sums[...] = jnp.zeros_like(sums)

    def fill(start, buffers):
        phases(start, scale, local, *buffers)

    def add(start, buffers):
        add_products(id_at + start, ids_ref, buffers[0], buffers[1], sums)

    fill(0, even)

    def two_batches(trip, carry):
        start = trip * 2 * step
        add(start, even)
        fill(start + step, odd)
        add(start + step, odd)
        fill(start + 2 * step, even)
        return carry

    trips = blocks // (2 * step) - 1
    lax.fori_loop(0, trips, two_batches, 0)
    add(trips * 2 * step, even)
    fill((trips * 2 + 1) * step, odd)
    add((trips * 2 + 1) * step, odd)

    owners = keep_ref.shape[0]
    pairs = sums.shape[0] // ROWS // owners // 2
    sign = sign_ref[0]
    low = lax.broadcasted_iota(jnp.int32, (1, LANES), 1) < LANES // 2

    def store(owner, rows, one, two):
        one_back, two_back = pltpu.roll(one, LANES // 2, 1), pltpu.roll(two, LANES // 2, 1)
        own = jnp.where(low, one_back + sign * one, two + sign * two_back)
        other = jnp.where(low, one - sign * one_back, two_back - sign * two)
        keep_ref[owner, rows, :] = own.astype(keep_ref.dtype)
        send_ref[owner, rows, :] = other.astype(send_ref.dtype)

    def store_owner(owner, carry):
        base = owner * (2 * pairs * ROWS)

        def rows_of(slot, row, count):
            return sums[pl.ds(pl.multiple_of(base + slot * ROWS + row, 8), count), :]

        for pair in range(pairs):
            store(
                owner, slice(pair * SUB, (pair + 1) * SUB), rows_of(pair, 0, SUB), rows_of(pairs + pair, 0, SUB)
            )
        blank = [jnp.zeros((16 - pairs, LANES), f32)]
        one = jnp.concatenate([rows_of(pair, SUB, 8)[:1] for pair in range(pairs)] + blank, axis=0)
        two = jnp.concatenate([rows_of(pairs + pair, SUB, 8)[:1] for pair in range(pairs)] + blank, axis=0)
        store(owner, slice(pairs * SUB, pairs * SUB + 16), one, two)
        return carry

    lax.fori_loop(0, owners, store_owner, 0)


def slot_sums(first, sign, block_slot, uv, mine, theirs, shard_count, slots):
    pairs = slots // 2
    rows = pairs * SUB + 16
    vmem = pl.BlockSpec(memory_space=pltpu.VMEM)
    smem = pl.BlockSpec(memory_space=pltpu.SMEM)
    buffers = [
        pltpu.VMEM((2, BATCH * 2 * PITCH * SUB + 16, LANES), f32),
        pltpu.VMEM((4, BATCH * 2 * GROUP, LANES), f32),
        pltpu.VMEM((3, 4 * GROUP + 8, LANES), f32),
    ]
    return pl.pallas_call(
        slot_sums_kernel,
        out_shape=[
            jax.ShapeDtypeStruct((shard_count, rows, LANES), f32),
            jax.ShapeDtypeStruct((shard_count, rows, LANES), bf16),
        ],
        in_specs=[smem, smem, smem, vmem, vmem, vmem],
        out_specs=[vmem, vmem],
        scratch_shapes=[pltpu.VMEM((shard_count * slots * ROWS, LANES), f32)]
        + buffers
        + buffers,
        compiler_params=pltpu.CompilerParams(vmem_limit_bytes=32 * 1024 * 1024),
        cost_estimate=pl.CostEstimate(flops=60_000_000_000, bytes_accessed=4_000_000, transcendentals=0),
        name="slot_sums",
    )(first, sign, block_slot, uv, mine, theirs)


def row_order():
    return np.array(list(range(HALF + 1, SUB)) + [HALF] + list(range(HALF - 1, -1, -1)))


def column_order():
    return np.array(list(range(HALF, SUB)) + list(range(HALF - 1, -1, -1)))


def dft_matrix():
    centred = np.arange(SUB) - HALF
    product_mod = centred[:, None] * centred[None, :] % SUB
    return np.exp(-2j * np.pi * product_mod / SUB) / math.sqrt(SUB)


def spread(matrix):
    parts = []
    for factor in (1, 1j):
        scaled = matrix * factor
        one = np.concatenate([scaled.real, scaled.imag], axis=1)
        parts.append(np.kron(np.eye(2), one))
    return np.concatenate(parts, axis=1).astype(np.float32)


def constants():
    rows_at, cols_at = row_order(), column_order()
    dft = dft_matrix()
    cols = dft.T[cols_at]
    columns = spread(np.concatenate([cols, 1j * cols], axis=0))
    rows = dft[:, rows_at]
    rows = np.concatenate([rows.real, rows.imag], axis=1).astype(np.float32)

    def outer(values):
        return values[rows_at][:, None], values[cols_at][None, :]

    place_x, place_y = outer((np.arange(SUB) - HALF) / SUB)
    taper_x, taper_y = outer(np.sin(np.pi * (np.arange(SUB) + 0.5) / SUB))
    n_term = np.sqrt(1.0 - place_x**2 - place_y**2) - 1.0
    turns = np.tile(-W_STEP * n_term, (1, 4)).astype(np.float32)
    tapers = np.tile(taper_x * taper_y, (1, 4)).astype(np.float32)

    def split(matrix):
        high = matrix.astype(jnp.bfloat16)
        return np.stack([high, (matrix - high.astype(np.float32)).astype(jnp.bfloat16)])

    return turns, tapers, split(columns), split(rows)


def halves(values):
    high = values.astype(bf16)
    return high, (values - high.astype(f32)).astype(bf16)


def dot_in_halves(left, right):
    (a, b), (c, d) = left, right
    small = jnp.dot(b, c, preferred_element_type=f32) + jnp.dot(a, d, preferred_element_type=f32)
    return small + jnp.dot(a, c, preferred_element_type=f32)


def transform_kernel(planes_ref, corners_ref, turns_ref, tapers_ref, columns_ref, rows_ref, *refs):
    sum_refs, out_ref = refs[:-1], refs[-1]
    pairs = out_ref.shape[0] // SUB
    plain = sum_refs[0][...].astype(f32)
    for sum_ref in sum_refs[1:]:
        plain = plain + sum_ref[...].astype(f32)
    lane = lax.broadcasted_iota(jnp.int32, (1, LANES), 1)
    turned = jnp.where(
        (lane // SUB) % 2 == 0, -pltpu.roll(plain, LANES - SUB, 1), pltpu.roll(plain, SUB, 1)
    )
    last = lax.broadcasted_iota(jnp.int32, (HALF, LANES), 0) == HALF - 1
    pieces = []
    for pair in range(pairs):
        at = pair * SUB
        cos_p, sin_p = plain[at : at + HALF], plain[at + HALF : at + SUB]
        cos_t, sin_t = turned[at : at + HALF], turned[at + HALF : at + SUB]
        zero = pairs * SUB + pair
        up = jnp.where(last, plain[zero : zero + 1], cos_p + sin_t)
        up_i = jnp.where(last, turned[zero : zero + 1], cos_t - sin_p)
        image = jnp.concatenate([up, cos_p - sin_t], axis=0)
        image_i = jnp.concatenate([up_i, cos_t + sin_p], axis=0)
        plane = jnp.where(lane < LANES // 2, planes_ref[pair], planes_ref[pairs + pair]).astype(f32)
        turns = plane * turns_ref[...]
        c_half, s_half = cos_sin((turns - jnp.floor(turns + 0.5)) * math.pi, 7)
        screen_cos = (1.0 - 2.0 * s_half * s_half) * tapers_ref[...]
        screen_sin = (2.0 * s_half * c_half) * tapers_ref[...]
        pieces.append(image * screen_cos + image_i * screen_sin)
    both = dot_in_halves(halves(jnp.concatenate(pieces, axis=0)), (columns_ref[0], columns_ref[1]))
    stacked = jnp.concatenate(
        [
            jnp.concatenate([both[pair * SUB : (pair + 1) * SUB, part : part + LANES] for pair in range(pairs)], axis=1)
            for part in (0, LANES)
        ],
        axis=0,
    )
    result = dot_in_halves((rows_ref[0], rows_ref[1]), halves(stacked)).astype(out_ref.dtype)
    for pair in range(pairs):
        out_ref[pair * SUB : (pair + 1) * SUB, :] = result[:, pair * LANES : (pair + 1) * LANES]
    out_ref[pairs * SUB :, :] = corners_ref[...].astype(out_ref.dtype)


def corner_rows(corners):
    digits = jnp.stack([corners // 16, corners % 16], axis=1).reshape(1, -1).astype(f32)
    return jnp.pad(digits, ((0, 15), (0, LANES - digits.shape[1])))


def subgrid_transform(sums, planes, corners, slots):
    vmem = pl.BlockSpec(memory_space=pltpu.VMEM)
    smem = pl.BlockSpec(memory_space=pltpu.SMEM)
    return pl.pallas_call(
        transform_kernel,
        out_shape=jax.ShapeDtypeStruct((slots // 2 * SUB + 16, LANES), bf16),
        in_specs=[smem] + [vmem] * (5 + len(sums)),
        out_specs=vmem,
        compiler_params=pltpu.CompilerParams(vmem_limit_bytes=32 * 1024 * 1024),
        name="subgrid_transform",
    )(planes, corner_rows(corners), *constants(), *sums)


def place_kernel(first, final, count, origin_ref, *refs):
    sub_refs = refs[:count]
    if final:
        out_ref, strip, decoded, corners, sem = refs[-5:]
    else:
        strip, decoded, corners, sem = refs[-4:]
    pairs = sub_refs[0].shape[0] // SUB
    slots = 2 * pairs
    for source, sub_ref in enumerate(sub_refs):
        digits = sub_ref[pairs * SUB :, :].astype(f32)
        joined = 16.0 * digits + pltpu.roll(digits, LANES - slots, 1)
        decoded[source * 8 : source * 8 + 8, :] = joined[:8].astype(jnp.int32)
    fetch = pltpu.make_async_copy(decoded, corners, sem.at[0, 0])
    fetch.start()
    if first:
        strip[...] = jnp.zeros_like(strip)
    lane = lax.broadcasted_iota(jnp.int32, (SUB, LANES), 1)
    cols = (strip.shape[1] - 2) * LANES
    fetch.wait()

    for source, sub_ref in enumerate(sub_refs):

        def add_pair(pair, carry, source=source, sub_ref=sub_ref):
            for half in range(2):
                row = corners[source * 8, half * pairs + pair] - origin_ref[0]
                col = corners[source * 8, 2 * slots + half * pairs + pair] - origin_ref[1]

                @pl.when((col > -SUB) & (col < cols))
                def _():
                    padded = col + LANES
                    tile = padded // LANES
                    at = padded % LANES
                    piece = sub_ref[pl.ds(pl.multiple_of(pair * SUB, SUB), SUB), :].astype(f32)
                    left = (lane >= at) & (lane < at + SUB)
                    right = lane < at + SUB - LANES
                    rows = pl.ds(row, SUB)
                    turned = [
                        pltpu.roll(piece, (at + (LANES - half * 2 * SUB - part * SUB)) % LANES, 1) for part in range(2)
                    ]
                    sums = [
                        strip[part, tile + over, rows, :] + jnp.where(mask, turned[part], 0.0)
                        for part in range(2)
                        for over, mask in enumerate((left, right))
                    ]
                    for part in range(2):
                        for over in range(2):
                            strip[part, tile + over, rows, :] = sums[2 * part + over]

            return carry

        lax.fori_loop(0, pairs, add_pair, 0)

    if final:
        copies = [
            pltpu.make_async_copy(
                strip.at[part, tile + 1, pl.ds(0, out_ref.shape[1]), :],
                out_ref.at[part, :, pl.ds(tile * LANES, LANES)],
                sem.at[part, tile],
            )
            for part in range(2)
            for tile in range(cols // LANES)
        ]
        for copy in copies:
            copy.start()
        for copy in copies:
            copy.wait()


def place(origin, subs, strip_rows, cols):
    smem = pl.BlockSpec(memory_space=pltpu.SMEM)
    vmem = pl.BlockSpec(memory_space=pltpu.VMEM)
    tiles = cols // LANES
    strip_shape = jax.ShapeDtypeStruct((2, tiles + 2, strip_rows + 8, LANES), f32)
    result = []
    for first, group in ((True, subs[:1]), (False, subs[1:])):
        outs, specs = [strip_shape], [vmem]
        if not first:
            outs = [jax.ShapeDtypeStruct((2, strip_rows, cols), f32)] + outs
            specs = [pl.BlockSpec(memory_space=pl.ANY)] + specs
        result = pl.pallas_call(
            functools.partial(place_kernel, first, not first, len(group)),
            out_shape=outs,
            in_specs=[smem] + [vmem] * (len(group) + len(result)),
            out_specs=specs,
            scratch_shapes=[
                pltpu.VMEM((8 * len(group), LANES), jnp.int32),
                pltpu.SMEM((8 * len(group), LANES), jnp.int32),
                pltpu.SemaphoreType.DMA((2, tiles)),
            ],
            input_output_aliases={} if first else {1 + len(group): 1},
            compiler_params=pltpu.CompilerParams(vmem_limit_bytes=32 * 1024 * 1024),
            name="place_own" if first else "place_others",
        )(origin, *group, *result)
    return result[0]


def around(block, axis):
    count = lax.axis_size(axis)
    return [block] + [
        lax.ppermute(block, axis, [(i, (i + step) % count) for i in range(count)]) for step in range(1, count)
    ]


def exchange(blocks, axis):
    count = lax.axis_size(axis)
    me = lax.axis_index(axis)

    def block_for(step):
        return lax.dynamic_index_in_dim(blocks, me ^ step, 0, keepdims=False)

    return [block_for(0)] + [
        lax.ppermute(block_for(step), axis, [(i, i ^ step) for i in range(count)])
        for step in range(1, count)
    ]


def on_device(visibilities, uv_coords, block_slot, slot_table):
    shard_count = lax.axis_size("bl")
    chan_count = lax.axis_size("chan")
    my_shard = lax.axis_index("bl")
    my_chan = lax.axis_index("chan")
    my_pol = lax.axis_index("pol")
    blocks = uv_coords.shape[0]
    slots = slot_table.shape[1]
    half = blocks // 2
    strip_rows = G // shard_count
    cols = G // chan_count

    def rows_of(values):
        count = values.shape[0]
        return values.reshape(count, 2, VB // LANES, LANES).transpose(0, 2, 1, 3).reshape(count * 4, LANES)

    vis = rows_of(visibilities[0])
    def half_of(rows, which):
        return lax.dynamic_slice_in_dim(rows, which * (half * 4), half * 4, 0)

    theirs = lax.ppermute(half_of(vis, 1 - my_pol), "pol", [(0, 1), (1, 0)])
    sign = (1.0 - 2.0 * my_pol.astype(f32))[None]
    first = (my_shard * blocks + my_pol * half)[None]
    coords, mine = lax.optimization_barrier((rows_of(uv_coords), vis))
    coords, mine = half_of(coords, my_pol), half_of(mine, my_pol)
    keep, send = slot_sums(first, sign, block_slot, coords, mine, theirs, shard_count, slots)
    got = lax.ppermute(send, "pol", [(0, 1), (1, 0)])
    partial = (keep + got.astype(f32)).astype(bf16)
    parts = exchange(partial, "bl")
    subs = around(subgrid_transform(parts, slot_table[2], slot_table[:2], slots), "chan")
    origin = jnp.stack([my_shard * strip_rows, my_chan * cols])
    return place(origin, subs, strip_rows, cols)[None]


def solution(mesh):
    return jax.shard_map(
        on_device,
        mesh=mesh,
        in_specs=(
            P("pol", ("chan", "bl"), None, None),
            P(("chan", "bl"), None, None),
            P("chan"),
            P(None, ("chan", "bl")),
        ),
        out_specs=P("pol", None, "bl", "chan"),
        check_vma=False,
    )
```

```python
import functools
import math

import jax
import jax.numpy as jnp
import numpy as np
from jax import lax
from jax.experimental import pallas as pl
from jax.experimental.pallas import tpu as pltpu
from jax.sharding import PartitionSpec as P

G = 2048
SUB = 32
VB = 256
HALF = SUB // 2
LANES = 128
ROWS = 40
W_STEP = 0.25
f32 = jnp.float32
bf16 = jnp.bfloat16


def cos_sin(angle, terms):
    square = angle * angle
    cos_sum = f32((-1.0) ** (terms - 1) / math.factorial(2 * terms - 2))
    sin_sum = f32((-1.0) ** (terms - 1) / math.factorial(2 * terms - 1))
    for n in range(terms - 2, -1, -1):
        cos_sum = cos_sum * square + f32((-1.0) ** n / math.factorial(2 * n))
        sin_sum = sin_sum * square + f32((-1.0) ** n / math.factorial(2 * n + 1))
    return cos_sum, sin_sum * angle


def multiples(coords):
    c_half, s_half = cos_sin(coords * (math.pi / SUB), 6)
    cosines = {1: 1.0 - 2.0 * s_half * s_half}
    sines = {1: 2.0 * s_half * c_half}
    for k in range(2, HALF + 1):
        base = 1 << ((k - 1).bit_length() - 1)
        twice = 2.0 * cosines[base]
        if k == 2 * base:
            cosines[k] = twice * cosines[base] - 1.0
            sines[k] = twice * sines[base]
        else:
            cosines[k] = twice * cosines[k - base] - cosines[2 * base - k]
            sines[k] = twice * sines[k - base] + sines[2 * base - k]
    return cosines, sines


def odd_halves(coords):
    c_half, s_half = cos_sin(coords * (math.pi / SUB), 6)
    twice = {1: 2.0 - 4.0 * s_half * s_half}
    for base in (2, 4, 8):
        twice[base] = twice[base // 2] * twice[base // 2] - 2.0
    cosines, sines = [c_half], [s_half]
    for j in range(1, HALF):
        base = 1 << (j.bit_length() - 1)
        cosines.append(twice[base] * cosines[j - base] - cosines[2 * base - 1 - j])
        sines.append(twice[base] * sines[j - base] + sines[2 * base - 1 - j])
    return cosines, sines


GROUP = 8
BATCH = 8
PITCH = 9


def phases(start, scale, inputs, angles, values, wide):
    for group in range(BATCH):
        rows = pl.ds(pl.multiple_of((start + group * GROUP) * 4, 4 * GROUP), 4 * GROUP)
        for which, ref in enumerate(inputs):
            wide[which, : 4 * GROUP, :] = ref[rows, :].astype(f32)
        for part in range(2):
            at = (group * 2 + part) * PITCH * SUB

            def pick(which, component):
                return wide[which, pl.ds(part * 16 + component, 8, 2), :]

            def put(side, number, value):
                angles[side, at + number * PITCH : at + number * PITCH + 8, :] = value

            cosines, sines = multiples(pick(0, 0))
            for k in range(1, HALF + 1):
                put(0, k - 1, cosines[k])
                put(0, HALF + k - 1, sines[k])
            cosines, sines = odd_halves(pick(0, 1))
            for k in range(HALF):
                put(1, k, cosines[k])
                put(1, HALF + k, sines[k])
            c_half, s_half = cosines[0] * scale, sines[0] * scale
            chunks = slice((group * 2 + part) * 8, (group * 2 + part + 1) * 8)
            for product in range(2):
                real, imag = pick(1 + product, 0), pick(1 + product, 1)
                values[2 * product, chunks, :] = real * c_half + imag * s_half
                values[2 * product + 1, chunks, :] = imag * c_half - real * s_half


def add_products(id_at, ids_ref, angles, values, sums):
    ones = jnp.ones((HALF, VB), bf16)
    for block in range(BATCH * GROUP):
        lefts, rights = [], []
        for chunk in (2 * block, 2 * block + 1):
            at = pl.ds(chunk // 8 * PITCH * SUB + chunk % 8, SUB, PITCH)
            lefts.append(angles[0, at, :].astype(bf16))
            phase = angles[1, at, :]
            cosine, sine = phase[:HALF], phase[HALF:]
            pieces = []
            for product in range(2):
                real = values[2 * product, chunk : chunk + 1, :]
                imag = values[2 * product + 1, chunk : chunk + 1, :]
                rc, is_, rs, ic = real * cosine, imag * sine, real * sine, imag * cosine
                for piece in (rc - is_, rc + is_, ic + rs, ic - rs):
                    pieces.append(piece.astype(bf16))
            rights.append(jnp.concatenate(pieces, axis=0))
        image = lax.dot_general(
            jnp.concatenate([jnp.concatenate(lefts, axis=1), ones], axis=0),
            jnp.concatenate(rights, axis=1),
            (((1,), (1,)), ((), ())),
            preferred_element_type=f32,
        )
        at = pl.ds(pl.multiple_of(ids_ref[id_at + block] * ROWS, 8), ROWS)
        sums[at, :] += image[:ROWS]


def slot_sums_kernel(first_ref, sign_ref, ids_ref, uv_ref, mine_ref, theirs_ref, keep_ref, send_ref, sums, *scratch):
    local = (uv_ref, mine_ref, theirs_ref)
    blocks = uv_ref.shape[0] // 4
    step = BATCH * GROUP
    id_at = first_ref[0]
    scale = 0.5 / math.sqrt(VB)
    even, odd = scratch[:3], scratch[3:]
    sums[...] = jnp.zeros_like(sums)

    def fill(start, buffers):
        phases(start, scale, local, *buffers)

    def add(start, buffers):
        add_products(id_at + start, ids_ref, buffers[0], buffers[1], sums)

    fill(0, even)

    def two_batches(trip, carry):
        start = trip * 2 * step
        add(start, even)
        fill(start + step, odd)
        add(start + step, odd)
        fill(start + 2 * step, even)
        return carry

    trips = blocks // (2 * step) - 1
    lax.fori_loop(0, trips, two_batches, 0)
    add(trips * 2 * step, even)
    fill((trips * 2 + 1) * step, odd)
    add((trips * 2 + 1) * step, odd)

    owners = keep_ref.shape[0]
    pairs = sums.shape[0] // ROWS // owners // 2
    sign = sign_ref[0]
    low = lax.broadcasted_iota(jnp.int32, (1, LANES), 1) < LANES // 2

    def store(owner, rows, one, two):
        one_back, two_back = pltpu.roll(one, LANES // 2, 1), pltpu.roll(two, LANES // 2, 1)
        own = jnp.where(low, one_back + sign * one, two + sign * two_back)
        other = jnp.where(low, one - sign * one_back, two_back - sign * two)
        keep_ref[owner, rows, :] = own.astype(keep_ref.dtype)
        send_ref[owner, rows, :] = other.astype(send_ref.dtype)

    def store_owner(owner, carry):
        base = owner * (2 * pairs * ROWS)

        def rows_of(slot, row, count):
            return sums[pl.ds(pl.multiple_of(base + slot * ROWS + row, 8), count), :]

        for pair in range(pairs):
            store(
                owner, slice(pair * SUB, (pair + 1) * SUB), rows_of(pair, 0, SUB), rows_of(pairs + pair, 0, SUB)
            )
        blank = [jnp.zeros((16 - pairs, LANES), f32)]
        one = jnp.concatenate([rows_of(pair, SUB, 8)[:1] for pair in range(pairs)] + blank, axis=0)
        two = jnp.concatenate([rows_of(pairs + pair, SUB, 8)[:1] for pair in range(pairs)] + blank, axis=0)
        store(owner, slice(pairs * SUB, pairs * SUB + 16), one, two)
        return carry

    lax.fori_loop(0, owners, store_owner, 0)


def slot_sums(first, sign, block_slot, uv, mine, theirs, shard_count, slots):
    pairs = slots // 2
    rows = pairs * SUB + 16
    vmem = pl.BlockSpec(memory_space=pltpu.VMEM)
    smem = pl.BlockSpec(memory_space=pltpu.SMEM)
    buffers = [
        pltpu.VMEM((2, BATCH * 2 * PITCH * SUB + 16, LANES), f32),
        pltpu.VMEM((4, BATCH * 2 * GROUP, LANES), f32),
        pltpu.VMEM((3, 4 * GROUP + 8, LANES), f32),
    ]
    return pl.pallas_call(
        slot_sums_kernel,
        out_shape=[
            jax.ShapeDtypeStruct((shard_count, rows, LANES), f32),
            jax.ShapeDtypeStruct((shard_count, rows, LANES), bf16),
        ],
        in_specs=[smem, smem, smem, vmem, vmem, vmem],
        out_specs=[vmem, vmem],
        scratch_shapes=[pltpu.VMEM((shard_count * slots * ROWS, LANES), f32)]
        + buffers
        + buffers,
        compiler_params=pltpu.CompilerParams(vmem_limit_bytes=32 * 1024 * 1024),
        cost_estimate=pl.CostEstimate(flops=60_000_000_000, bytes_accessed=4_000_000, transcendentals=0),
        name="slot_sums",
    )(first, sign, block_slot, uv, mine, theirs)


def row_order():
    return np.array(list(range(HALF + 1, SUB)) + [HALF] + list(range(HALF - 1, -1, -1)))


def column_order():
    return np.array(list(range(HALF, SUB)) + list(range(HALF - 1, -1, -1)))


def dft_matrix():
    centred = np.arange(SUB) - HALF
    product_mod = centred[:, None] * centred[None, :] % SUB
    return np.exp(-2j * np.pi * product_mod / SUB) / math.sqrt(SUB)


def spread(matrix):
    parts = []
    for factor in (1, 1j):
        scaled = matrix * factor
        one = np.concatenate([scaled.real, scaled.imag], axis=1)
        parts.append(np.kron(np.eye(2), one))
    return np.concatenate(parts, axis=1).astype(np.float32)


def constants():
    rows_at, cols_at = row_order(), column_order()
    dft = dft_matrix()
    cols = dft.T[cols_at]
    columns = spread(np.concatenate([cols, 1j * cols], axis=0))
    rows = dft[:, rows_at]
    rows = np.concatenate([rows.real, rows.imag], axis=1).astype(np.float32)

    def outer(values):
        return values[rows_at][:, None], values[cols_at][None, :]

    place_x, place_y = outer((np.arange(SUB) - HALF) / SUB)
    taper_x, taper_y = outer(np.sin(np.pi * (np.arange(SUB) + 0.5) / SUB))
    n_term = np.sqrt(1.0 - place_x**2 - place_y**2) - 1.0
    turns = np.tile(-W_STEP * n_term, (1, 4)).astype(np.float32)
    tapers = np.tile(taper_x * taper_y, (1, 4)).astype(np.float32)

    def split(matrix):
        high = matrix.astype(jnp.bfloat16)
        return np.stack([high, (matrix - high.astype(np.float32)).astype(jnp.bfloat16)])

    return turns, tapers, split(columns), split(rows)


def halves(values):
    high = values.astype(bf16)
    return high, (values - high.astype(f32)).astype(bf16)


def dot_in_halves(left, right):
    (a, b), (c, d) = left, right
    small = jnp.dot(b, c, preferred_element_type=f32) + jnp.dot(a, d, preferred_element_type=f32)
    return small + jnp.dot(a, c, preferred_element_type=f32)


def transform_kernel(planes_ref, corners_ref, turns_ref, tapers_ref, columns_ref, rows_ref, *refs):
    sum_refs, out_ref = refs[:-1], refs[-1]
    pairs = out_ref.shape[0] // SUB
    plain = sum_refs[0][...].astype(f32)
    for sum_ref in sum_refs[1:]:
        plain = plain + sum_ref[...].astype(f32)
    lane = lax.broadcasted_iota(jnp.int32, (1, LANES), 1)
    turned = jnp.where(
        (lane // SUB) % 2 == 0, -pltpu.roll(plain, LANES - SUB, 1), pltpu.roll(plain, SUB, 1)
    )
    last = lax.broadcasted_iota(jnp.int32, (HALF, LANES), 0) == HALF - 1
    pieces = []
    for pair in range(pairs):
        at = pair * SUB
        cos_p, sin_p = plain[at : at + HALF], plain[at + HALF : at + SUB]
        cos_t, sin_t = turned[at : at + HALF], turned[at + HALF : at + SUB]
        zero = pairs * SUB + pair
        up = jnp.where(last, plain[zero : zero + 1], cos_p + sin_t)
        up_i = jnp.where(last, turned[zero : zero + 1], cos_t - sin_p)
        image = jnp.concatenate([up, cos_p - sin_t], axis=0)
        image_i = jnp.concatenate([up_i, cos_t + sin_p], axis=0)
        plane = jnp.where(lane < LANES // 2, planes_ref[pair], planes_ref[pairs + pair]).astype(f32)
        turns = plane * turns_ref[...]
        c_half, s_half = cos_sin((turns - jnp.floor(turns + 0.5)) * math.pi, 7)
        screen_cos = (1.0 - 2.0 * s_half * s_half) * tapers_ref[...]
        screen_sin = (2.0 * s_half * c_half) * tapers_ref[...]
        pieces.append(image * screen_cos + image_i * screen_sin)
    both = dot_in_halves(halves(jnp.concatenate(pieces, axis=0)), (columns_ref[0], columns_ref[1]))
    stacked = jnp.concatenate(
        [
            jnp.concatenate([both[pair * SUB : (pair + 1) * SUB, part : part + LANES] for pair in range(pairs)], axis=1)
            for part in (0, LANES)
        ],
        axis=0,
    )
    result = dot_in_halves((rows_ref[0], rows_ref[1]), halves(stacked)).astype(out_ref.dtype)
    for pair in range(pairs):
        out_ref[pair * SUB : (pair + 1) * SUB, :] = result[:, pair * LANES : (pair + 1) * LANES]
    out_ref[pairs * SUB :, :] = corners_ref[...].astype(out_ref.dtype)


def corner_rows(corners):
    digits = jnp.stack([corners // 16, corners % 16], axis=1).reshape(1, -1).astype(f32)
    return jnp.pad(digits, ((0, 15), (0, LANES - digits.shape[1])))


def subgrid_transform(sums, planes, corners, slots):
    vmem = pl.BlockSpec(memory_space=pltpu.VMEM)
    smem = pl.BlockSpec(memory_space=pltpu.SMEM)
    return pl.pallas_call(
        transform_kernel,
        out_shape=jax.ShapeDtypeStruct((slots // 2 * SUB + 16, LANES), bf16),
        in_specs=[smem] + [vmem] * (5 + len(sums)),
        out_specs=vmem,
        compiler_params=pltpu.CompilerParams(vmem_limit_bytes=32 * 1024 * 1024),
        name="subgrid_transform",
    )(planes, corner_rows(corners), *constants(), *sums)


def place_kernel(first, final, count, origin_ref, *refs):
    sub_refs = refs[:count]
    if final:
        out_ref, strip, decoded, corners, sem = refs[-5:]
    else:
        strip, decoded, corners, sem = refs[-4:]
    pairs = sub_refs[0].shape[0] // SUB
    slots = 2 * pairs
    for source, sub_ref in enumerate(sub_refs):
        digits = sub_ref[pairs * SUB :, :].astype(f32)
        joined = 16.0 * digits + pltpu.roll(digits, LANES - slots, 1)
        decoded[source * 8 : source * 8 + 8, :] = joined[:8].astype(jnp.int32)
    fetch = pltpu.make_async_copy(decoded, corners, sem.at[0, 0])
    fetch.start()
    if first:
        strip[...] = jnp.zeros_like(strip)
    lane = lax.broadcasted_iota(jnp.int32, (SUB, LANES), 1)
    cols = (strip.shape[1] - 2) * LANES
    fetch.wait()

    for source, sub_ref in enumerate(sub_refs):

        def add_pair(pair, carry, source=source, sub_ref=sub_ref):
            for half in range(2):
                row = corners[source * 8, half * pairs + pair] - origin_ref[0]
                col = corners[source * 8, 2 * slots + half * pairs + pair] - origin_ref[1]

                @pl.when((col > -SUB) & (col < cols))
                def _():
                    padded = col + LANES
                    tile = padded // LANES
                    at = padded % LANES
                    piece = sub_ref[pl.ds(pl.multiple_of(pair * SUB, SUB), SUB), :].astype(f32)
                    left = (lane >= at) & (lane < at + SUB)
                    right = lane < at + SUB - LANES
                    rows = pl.ds(row, SUB)
                    turned = [
                        pltpu.roll(piece, (at + (LANES - half * 2 * SUB - part * SUB)) % LANES, 1) for part in range(2)
                    ]
                    sums = [
                        strip[part, tile + over, rows, :] + jnp.where(mask, turned[part], 0.0)
                        for part in range(2)
                        for over, mask in enumerate((left, right))
                    ]
                    for part in range(2):
                        for over in range(2):
                            strip[part, tile + over, rows, :] = sums[2 * part + over]

            return carry

        lax.fori_loop(0, pairs, add_pair, 0)

    if final:
        copies = [
            pltpu.make_async_copy(
                strip.at[part, tile + 1, pl.ds(0, out_ref.shape[1]), :],
                out_ref.at[part, :, pl.ds(tile * LANES, LANES)],
                sem.at[part, tile],
            )
            for part in range(2)
            for tile in range(cols // LANES)
        ]
        for copy in copies:
            copy.start()
        for copy in copies:
            copy.wait()


def place(origin, subs, strip_rows, cols):
    smem = pl.BlockSpec(memory_space=pltpu.SMEM)
    vmem = pl.BlockSpec(memory_space=pltpu.VMEM)
    tiles = cols // LANES
    strip_shape = jax.ShapeDtypeStruct((2, tiles + 2, strip_rows + 8, LANES), f32)
    result = []
    for first, group in ((True, subs[:1] + subs[-1:]), (False, subs[1:-1])):
        outs, specs = [strip_shape], [vmem]
        if not first:
            outs = [jax.ShapeDtypeStruct((2, strip_rows, cols), f32)] + outs
            specs = [pl.BlockSpec(memory_space=pl.ANY)] + specs
        result = pl.pallas_call(
            functools.partial(place_kernel, first, not first, len(group)),
            out_shape=outs,
            in_specs=[smem] + [vmem] * (len(group) + len(result)),
            out_specs=specs,
            scratch_shapes=[
                pltpu.VMEM((8 * len(group), LANES), jnp.int32),
                pltpu.SMEM((8 * len(group), LANES), jnp.int32),
                pltpu.SemaphoreType.DMA((2, tiles)),
            ],
            input_output_aliases={} if first else {1 + len(group): 1},
            compiler_params=pltpu.CompilerParams(vmem_limit_bytes=32 * 1024 * 1024),
            name="place_own" if first else "place_others",
        )(origin, *group, *result)
    return result[0]


def around(block, axis):
    count = lax.axis_size(axis)
    return [block] + [
        lax.ppermute(block, axis, [(i, (i + step) % count) for i in range(count)]) for step in range(1, count)
    ]


def exchange(blocks, axis):
    count = lax.axis_size(axis)
    me = lax.axis_index(axis)

    def block_for(step):
        return lax.dynamic_index_in_dim(blocks, me ^ step, 0, keepdims=False)

    return [block_for(0)] + [
        lax.ppermute(block_for(step), axis, [(i, i ^ step) for i in range(count)])
        for step in range(1, count)
    ]


def on_device(visibilities, uv_coords, block_slot, slot_table):
    shard_count = lax.axis_size("bl")
    chan_count = lax.axis_size("chan")
    my_shard = lax.axis_index("bl")
    my_chan = lax.axis_index("chan")
    my_pol = lax.axis_index("pol")
    blocks = uv_coords.shape[0]
    slots = slot_table.shape[1]
    half = blocks // 2
    strip_rows = G // shard_count
    cols = G // chan_count

    def rows_of(values):
        count = values.shape[0]
        return values.reshape(count, 2, VB // LANES, LANES).transpose(0, 2, 1, 3).reshape(count * 4, LANES)

    vis = rows_of(visibilities[0])
    def half_of(rows, which):
        return lax.dynamic_slice_in_dim(rows, which * (half * 4), half * 4, 0)

    theirs = lax.ppermute(half_of(vis, 1 - my_pol), "pol", [(0, 1), (1, 0)])
    sign = (1.0 - 2.0 * my_pol.astype(f32))[None]
    first = (my_shard * blocks + my_pol * half)[None]
    coords, mine = lax.optimization_barrier((rows_of(uv_coords), vis))
    coords, mine = half_of(coords, my_pol), half_of(mine, my_pol)
    keep, send = slot_sums(first, sign, block_slot, coords, mine, theirs, shard_count, slots)
    got = lax.ppermute(send, "pol", [(0, 1), (1, 0)])
    partial = (keep + got.astype(f32)).astype(bf16)
    parts = exchange(partial, "bl")
    subs = around(subgrid_transform(parts, slot_table[2], slot_table[:2], slots), "chan")
    origin = jnp.stack([my_shard * strip_rows, my_chan * cols])
    return place(origin, subs, strip_rows, cols)[None]


def solution(mesh):
    return jax.shard_map(
        on_device,
        mesh=mesh,
        in_specs=(
            P("pol", ("chan", "bl"), None, None),
            P(("chan", "bl"), None, None),
            P("chan"),
            P(None, ("chan", "bl")),
        ),
        out_specs=P("pol", None, "bl", "chan"),
        check_vma=False,
    )
```

```python
import functools
import math

import jax
import jax.numpy as jnp
import numpy as np
from jax import lax
from jax.experimental import pallas as pl
from jax.experimental.pallas import tpu as pltpu
from jax.sharding import PartitionSpec as P

G = 2048
SUB = 32
VB = 256
HALF = SUB // 2
LANES = 128
ROWS = 40
W_STEP = 0.25
f32 = jnp.float32
bf16 = jnp.bfloat16


def cos_sin(angle, terms):
    square = angle * angle
    cos_sum = f32((-1.0) ** (terms - 1) / math.factorial(2 * terms - 2))
    sin_sum = f32((-1.0) ** (terms - 1) / math.factorial(2 * terms - 1))
    for n in range(terms - 2, -1, -1):
        cos_sum = cos_sum * square + f32((-1.0) ** n / math.factorial(2 * n))
        sin_sum = sin_sum * square + f32((-1.0) ** n / math.factorial(2 * n + 1))
    return cos_sum, sin_sum * angle


def multiples(coords):
    c_half, s_half = cos_sin(coords * (math.pi / SUB), 6)
    cosines = {1: 1.0 - 2.0 * s_half * s_half}
    sines = {1: 2.0 * s_half * c_half}
    for k in range(2, HALF + 1):
        base = 1 << ((k - 1).bit_length() - 1)
        twice = 2.0 * cosines[base]
        if k == 2 * base:
            cosines[k] = twice * cosines[base] - 1.0
            sines[k] = twice * sines[base]
        else:
            cosines[k] = twice * cosines[k - base] - cosines[2 * base - k]
            sines[k] = twice * sines[k - base] + sines[2 * base - k]
    return cosines, sines


def odd_halves(coords):
    c_half, s_half = cos_sin(coords * (math.pi / SUB), 6)
    twice = {1: 2.0 - 4.0 * s_half * s_half}
    for base in (2, 4, 8):
        twice[base] = twice[base // 2] * twice[base // 2] - 2.0
    cosines, sines = [c_half], [s_half]
    for j in range(1, HALF):
        base = 1 << (j.bit_length() - 1)
        cosines.append(twice[base] * cosines[j - base] - cosines[2 * base - 1 - j])
        sines.append(twice[base] * sines[j - base] + sines[2 * base - 1 - j])
    return cosines, sines


GROUP = 8
BATCH = 8
PITCH = 9


def phases(start, scale, inputs, angles, values, wide):
    for group in range(BATCH):
        rows = pl.ds(pl.multiple_of((start + group * GROUP) * 4, 4 * GROUP), 4 * GROUP)
        for which, ref in enumerate(inputs):
            wide[which, : 4 * GROUP, :] = ref[rows, :].astype(f32)
        for part in range(2):
            at = (group * 2 + part) * PITCH * SUB

            def pick(which, component):
                return wide[which, pl.ds(part * 16 + component, 8, 2), :]

            def put(side, number, value):
                angles[side, at + number * PITCH : at + number * PITCH + 8, :] = value

            cosines, sines = multiples(pick(0, 0))
            for k in range(1, HALF + 1):
                put(0, k - 1, cosines[k])
                put(0, HALF + k - 1, sines[k])
            cosines, sines = odd_halves(pick(0, 1))
            for k in range(HALF):
                put(1, k, cosines[k])
                put(1, HALF + k, sines[k])
            c_half, s_half = cosines[0] * scale, sines[0] * scale
            chunks = slice((group * 2 + part) * 8, (group * 2 + part + 1) * 8)
            for product in range(2):
                real, imag = pick(1 + product, 0), pick(1 + product, 1)
                values[2 * product, chunks, :] = real * c_half + imag * s_half
                values[2 * product + 1, chunks, :] = imag * c_half - real * s_half


def add_products(id_at, ids_ref, angles, values, sums):
    ones = jnp.ones((HALF, VB), bf16)
    for block in range(BATCH * GROUP):
        lefts, rights = [], []
        for chunk in (2 * block, 2 * block + 1):
            at = pl.ds(chunk // 8 * PITCH * SUB + chunk % 8, SUB, PITCH)
            lefts.append(angles[0, at, :].astype(bf16))
            phase = angles[1, at, :]
            cosine, sine = phase[:HALF], phase[HALF:]
            pieces = []
            for product in range(2):
                real = values[2 * product, chunk : chunk + 1, :]
                imag = values[2 * product + 1, chunk : chunk + 1, :]
                rc, is_, rs, ic = real * cosine, imag * sine, real * sine, imag * cosine
                for piece in (rc - is_, rc + is_, ic + rs, ic - rs):
                    pieces.append(piece.astype(bf16))
            rights.append(jnp.concatenate(pieces, axis=0))
        image = lax.dot_general(
            jnp.concatenate([jnp.concatenate(lefts, axis=1), ones], axis=0),
            jnp.concatenate(rights, axis=1),
            (((1,), (1,)), ((), ())),
            preferred_element_type=f32,
        )
        at = pl.ds(pl.multiple_of(ids_ref[id_at + block] * ROWS, 8), ROWS)
        sums[at, :] += image[:ROWS]


def slot_sums_kernel(first_ref, sign_ref, ids_ref, uv_ref, mine_ref, theirs_ref, keep_ref, send_ref, sums, *scratch):
    local = (uv_ref, mine_ref, theirs_ref)
    blocks = uv_ref.shape[0] // 4
    step = BATCH * GROUP
    id_at = first_ref[0]
    scale = 0.5 / math.sqrt(VB)
    even, odd = scratch[:3], scratch[3:]
    sums[...] = jnp.zeros_like(sums)

    def fill(start, buffers):
        phases(start, scale, local, *buffers)

    def add(start, buffers):
        add_products(id_at + start, ids_ref, buffers[0], buffers[1], sums)

    fill(0, even)

    def two_batches(trip, carry):
        start = trip * 2 * step
        add(start, even)
        fill(start + step, odd)
        add(start + step, odd)
        fill(start + 2 * step, even)
        return carry

    trips = blocks // (2 * step) - 1
    lax.fori_loop(0, trips, two_batches, 0)
    add(trips * 2 * step, even)
    fill((trips * 2 + 1) * step, odd)
    add((trips * 2 + 1) * step, odd)

    owners = keep_ref.shape[0]
    pairs = sums.shape[0] // ROWS // owners // 2
    sign = sign_ref[0]
    low = lax.broadcasted_iota(jnp.int32, (1, LANES), 1) < LANES // 2

    def store(owner, rows, one, two):
        one_back, two_back = pltpu.roll(one, LANES // 2, 1), pltpu.roll(two, LANES // 2, 1)
        own = jnp.where(low, one_back + sign * one, two + sign * two_back)
        other = jnp.where(low, one - sign * one_back, two_back - sign * two)
        keep_ref[owner, rows, :] = own.astype(keep_ref.dtype)
        send_ref[owner, rows, :] = other.astype(send_ref.dtype)

    def store_owner(owner, carry):
        base = owner * (2 * pairs * ROWS)

        def rows_of(slot, row, count):
            return sums[pl.ds(pl.multiple_of(base + slot * ROWS + row, 8), count), :]

        for pair in range(pairs):
            store(
                owner, slice(pair * SUB, (pair + 1) * SUB), rows_of(pair, 0, SUB), rows_of(pairs + pair, 0, SUB)
            )
        blank = [jnp.zeros((16 - pairs, LANES), f32)]
        one = jnp.concatenate([rows_of(pair, SUB, 8)[:1] for pair in range(pairs)] + blank, axis=0)
        two = jnp.concatenate([rows_of(pairs + pair, SUB, 8)[:1] for pair in range(pairs)] + blank, axis=0)
        store(owner, slice(pairs * SUB, pairs * SUB + 16), one, two)
        return carry

    lax.fori_loop(0, owners, store_owner, 0)


def slot_sums(first, sign, block_slot, uv, mine, theirs, shard_count, slots):
    pairs = slots // 2
    rows = pairs * SUB + 16
    vmem = pl.BlockSpec(memory_space=pltpu.VMEM)
    smem = pl.BlockSpec(memory_space=pltpu.SMEM)
    buffers = [
        pltpu.VMEM((2, BATCH * 2 * PITCH * SUB + 16, LANES), f32),
        pltpu.VMEM((4, BATCH * 2 * GROUP, LANES), f32),
        pltpu.VMEM((3, 4 * GROUP + 8, LANES), f32),
    ]
    return pl.pallas_call(
        slot_sums_kernel,
        out_shape=[
            jax.ShapeDtypeStruct((shard_count, rows, LANES), f32),
            jax.ShapeDtypeStruct((shard_count, rows, LANES), bf16),
        ],
        in_specs=[smem, smem, smem, vmem, vmem, vmem],
        out_specs=[vmem, vmem],
        scratch_shapes=[pltpu.VMEM((shard_count * slots * ROWS, LANES), f32)]
        + buffers
        + buffers,
        compiler_params=pltpu.CompilerParams(vmem_limit_bytes=32 * 1024 * 1024),
        cost_estimate=pl.CostEstimate(flops=60_000_000_000, bytes_accessed=4_000_000, transcendentals=0),
        name="slot_sums",
    )(first, sign, block_slot, uv, mine, theirs)


def row_order():
    return np.array(list(range(HALF + 1, SUB)) + [HALF] + list(range(HALF - 1, -1, -1)))


def column_order():
    return np.array(list(range(HALF, SUB)) + list(range(HALF - 1, -1, -1)))


def dft_matrix():
    centred = np.arange(SUB) - HALF
    product_mod = centred[:, None] * centred[None, :] % SUB
    return np.exp(-2j * np.pi * product_mod / SUB) / math.sqrt(SUB)


def spread(matrix):
    parts = []
    for factor in (1, 1j):
        scaled = matrix * factor
        one = np.concatenate([scaled.real, scaled.imag], axis=1)
        parts.append(np.kron(np.eye(2), one))
    return np.concatenate(parts, axis=1).astype(np.float32)


def constants():
    rows_at, cols_at = row_order(), column_order()
    dft = dft_matrix()
    cols = dft.T[cols_at]
    columns = spread(np.concatenate([cols, 1j * cols], axis=0))
    rows = dft[:, rows_at]
    rows = np.concatenate([rows.real, rows.imag], axis=1).astype(np.float32)

    def outer(values):
        return values[rows_at][:, None], values[cols_at][None, :]

    place_x, place_y = outer((np.arange(SUB) - HALF) / SUB)
    taper_x, taper_y = outer(np.sin(np.pi * (np.arange(SUB) + 0.5) / SUB))
    n_term = np.sqrt(1.0 - place_x**2 - place_y**2) - 1.0
    turns = np.tile(-W_STEP * n_term, (1, 4)).astype(np.float32)
    tapers = np.tile(taper_x * taper_y, (1, 4)).astype(np.float32)

    def split(matrix):
        high = matrix.astype(jnp.bfloat16)
        return np.stack([high, (matrix - high.astype(np.float32)).astype(jnp.bfloat16)])

    return turns, tapers, split(columns), split(rows)


def halves(values):
    high = values.astype(bf16)
    return high, (values - high.astype(f32)).astype(bf16)


def dot_in_halves(left, right):
    (a, b), (c, d) = left, right
    small = jnp.dot(b, c, preferred_element_type=f32) + jnp.dot(a, d, preferred_element_type=f32)
    return small + jnp.dot(a, c, preferred_element_type=f32)


def transform_kernel(planes_ref, corners_ref, turns_ref, tapers_ref, columns_ref, rows_ref, *refs):
    sum_refs, out_ref = refs[:-1], refs[-1]
    pairs = out_ref.shape[0] // SUB
    plain = sum_refs[0][...].astype(f32)
    for sum_ref in sum_refs[1:]:
        plain = plain + sum_ref[...].astype(f32)
    lane = lax.broadcasted_iota(jnp.int32, (1, LANES), 1)
    turned = jnp.where(
        (lane // SUB) % 2 == 0, -pltpu.roll(plain, LANES - SUB, 1), pltpu.roll(plain, SUB, 1)
    )
    last = lax.broadcasted_iota(jnp.int32, (HALF, LANES), 0) == HALF - 1
    pieces = []
    for pair in range(pairs):
        at = pair * SUB
        cos_p, sin_p = plain[at : at + HALF], plain[at + HALF : at + SUB]
        cos_t, sin_t = turned[at : at + HALF], turned[at + HALF : at + SUB]
        zero = pairs * SUB + pair
        up = jnp.where(last, plain[zero : zero + 1], cos_p + sin_t)
        up_i = jnp.where(last, turned[zero : zero + 1], cos_t - sin_p)
        image = jnp.concatenate([up, cos_p - sin_t], axis=0)
        image_i = jnp.concatenate([up_i, cos_t + sin_p], axis=0)
        plane = jnp.where(lane < LANES // 2, planes_ref[pair], planes_ref[pairs + pair]).astype(f32)
        turns = plane * turns_ref[...]
        c_half, s_half = cos_sin((turns - jnp.floor(turns + 0.5)) * math.pi, 7)
        screen_cos = (1.0 - 2.0 * s_half * s_half) * tapers_ref[...]
        screen_sin = (2.0 * s_half * c_half) * tapers_ref[...]
        pieces.append(image * screen_cos + image_i * screen_sin)
    both = dot_in_halves(halves(jnp.concatenate(pieces, axis=0)), (columns_ref[0], columns_ref[1]))
    stacked = jnp.concatenate(
        [
            jnp.concatenate([both[pair * SUB : (pair + 1) * SUB, part : part + LANES] for pair in range(pairs)], axis=1)
            for part in (0, LANES)
        ],
        axis=0,
    )
    result = dot_in_halves((rows_ref[0], rows_ref[1]), halves(stacked)).astype(out_ref.dtype)
    for pair in range(pairs):
        out_ref[pair * SUB : (pair + 1) * SUB, :] = result[:, pair * LANES : (pair + 1) * LANES]
    out_ref[pairs * SUB :, :] = corners_ref[...].astype(out_ref.dtype)


def corner_rows(corners):
    digits = jnp.stack([corners // 16, corners % 16], axis=1).reshape(1, -1).astype(f32)
    return jnp.pad(digits, ((0, 15), (0, LANES - digits.shape[1])))


def subgrid_transform(sums, planes, corners, slots):
    vmem = pl.BlockSpec(memory_space=pltpu.VMEM)
    smem = pl.BlockSpec(memory_space=pltpu.SMEM)
    return pl.pallas_call(
        transform_kernel,
        out_shape=jax.ShapeDtypeStruct((slots // 2 * SUB + 16, LANES), bf16),
        in_specs=[smem] + [vmem] * (5 + len(sums)),
        out_specs=vmem,
        compiler_params=pltpu.CompilerParams(vmem_limit_bytes=32 * 1024 * 1024),
        name="subgrid_transform",
    )(planes, corner_rows(corners), *constants(), *sums)


def place_kernel(first, final, count, origin_ref, *refs):
    sub_refs = refs[:count]
    if final:
        out_ref, strip, decoded, corners, sem = refs[-5:]
    else:
        strip, decoded, corners, sem = refs[-4:]
    pairs = sub_refs[0].shape[0] // SUB
    slots = 2 * pairs
    for source, sub_ref in enumerate(sub_refs):
        digits = sub_ref[pairs * SUB :, :].astype(f32)
        joined = 16.0 * digits + pltpu.roll(digits, LANES - slots, 1)
        decoded[source * 8 : source * 8 + 8, :] = joined[:8].astype(jnp.int32)
    fetch = pltpu.make_async_copy(decoded, corners, sem.at[0, 0])
    fetch.start()
    if first:
        strip[...] = jnp.zeros_like(strip)
    lane = lax.broadcasted_iota(jnp.int32, (SUB, LANES), 1)
    cols = (strip.shape[1] - 2) * LANES
    fetch.wait()

    for source, sub_ref in enumerate(sub_refs):

        def add_pair(pair, carry, source=source, sub_ref=sub_ref):
            for half in range(2):
                row = corners[source * 8, half * pairs + pair] - origin_ref[0]
                col = corners[source * 8, 2 * slots + half * pairs + pair] - origin_ref[1]

                @pl.when((col > -SUB) & (col < cols))
                def _():
                    padded = col + LANES
                    tile = padded // LANES
                    at = padded % LANES
                    piece = sub_ref[pl.ds(pl.multiple_of(pair * SUB, SUB), SUB), :].astype(f32)
                    left = (lane >= at) & (lane < at + SUB)
                    right = lane < at + SUB - LANES
                    rows = pl.ds(row, SUB)
                    turned = [
                        pltpu.roll(piece, (at + (LANES - half * 2 * SUB - part * SUB)) % LANES, 1) for part in range(2)
                    ]
                    sums = [
                        strip[part, tile + over, rows, :] + jnp.where(mask, turned[part], 0.0)
                        for part in range(2)
                        for over, mask in enumerate((left, right))
                    ]
                    for part in range(2):
                        for over in range(2):
                            strip[part, tile + over, rows, :] = sums[2 * part + over]

            return carry

        lax.fori_loop(0, pairs, add_pair, 0)

    if final:
        copies = [
            pltpu.make_async_copy(
                strip.at[part, tile + 1, pl.ds(0, out_ref.shape[1]), :],
                out_ref.at[part, :, pl.ds(tile * LANES, LANES)],
                sem.at[part, tile],
            )
            for part in range(2)
            for tile in range(cols // LANES)
        ]
        for copy in copies:
            copy.start()
        for copy in copies:
            copy.wait()


def place(origin, subs, strip_rows, cols):
    smem = pl.BlockSpec(memory_space=pltpu.SMEM)
    vmem = pl.BlockSpec(memory_space=pltpu.VMEM)
    tiles = cols // LANES
    strip_shape = jax.ShapeDtypeStruct((2, tiles + 2, strip_rows + 8, LANES), f32)
    result = []
    for first, group in ((True, subs[:1] + subs[-1:]), (False, subs[1:-1])):
        outs, specs = [strip_shape], [vmem]
        if not first:
            outs = [jax.ShapeDtypeStruct((2, strip_rows, cols), f32)] + outs
            specs = [pl.BlockSpec(memory_space=pl.ANY)] + specs
        result = pl.pallas_call(
            functools.partial(place_kernel, first, not first, len(group)),
            out_shape=outs,
            in_specs=[smem] + [vmem] * (len(group) + len(result)),
            out_specs=specs,
            scratch_shapes=[
                pltpu.VMEM((8 * len(group), LANES), jnp.int32),
                pltpu.SMEM((8 * len(group), LANES), jnp.int32),
                pltpu.SemaphoreType.DMA((2, tiles)),
            ],
            input_output_aliases={} if first else {1 + len(group): 1},
            compiler_params=pltpu.CompilerParams(vmem_limit_bytes=32 * 1024 * 1024),
            name="place_own" if first else "place_others",
        )(origin, *group, *result)
    return result[0]


def around(block, axis):
    count = lax.axis_size(axis)
    return [block] + [
        lax.ppermute(block, axis, [(i, i ^ step) for i in range(count)]) for step in range(1, count)
    ]


def exchange(blocks, axis):
    count = lax.axis_size(axis)
    me = lax.axis_index(axis)

    def block_for(step):
        return lax.dynamic_index_in_dim(blocks, me ^ step, 0, keepdims=False)

    return [block_for(0)] + [
        lax.ppermute(block_for(step), axis, [(i, i ^ step) for i in range(count)])
        for step in range(1, count)
    ]


def on_device(visibilities, uv_coords, block_slot, slot_table):
    shard_count = lax.axis_size("bl")
    chan_count = lax.axis_size("chan")
    my_shard = lax.axis_index("bl")
    my_chan = lax.axis_index("chan")
    my_pol = lax.axis_index("pol")
    blocks = uv_coords.shape[0]
    slots = slot_table.shape[1]
    half = blocks // 2
    strip_rows = G // shard_count
    cols = G // chan_count

    def rows_of(values):
        count = values.shape[0]
        return values.reshape(count, 2, VB // LANES, LANES).transpose(0, 2, 1, 3).reshape(count * 4, LANES)

    vis = rows_of(visibilities[0])
    def half_of(rows, which):
        return lax.dynamic_slice_in_dim(rows, which * (half * 4), half * 4, 0)

    theirs = lax.ppermute(half_of(vis, 1 - my_pol), "pol", [(0, 1), (1, 0)])
    sign = (1.0 - 2.0 * my_pol.astype(f32))[None]
    first = (my_shard * blocks + my_pol * half)[None]
    coords, mine = lax.optimization_barrier((rows_of(uv_coords), vis))
    coords, mine = half_of(coords, my_pol), half_of(mine, my_pol)
    keep, send = slot_sums(first, sign, block_slot, coords, mine, theirs, shard_count, slots)
    got = lax.ppermute(send, "pol", [(0, 1), (1, 0)])
    partial = (keep + got.astype(f32)).astype(bf16)
    parts = exchange(partial, "bl")
    subs = around(subgrid_transform(parts, slot_table[2], slot_table[:2], slots), "chan")
    origin = jnp.stack([my_shard * strip_rows, my_chan * cols])
    return place(origin, subs, strip_rows, cols)[None]


def solution(mesh):
    return jax.shard_map(
        on_device,
        mesh=mesh,
        in_specs=(
            P("pol", ("chan", "bl"), None, None),
            P(("chan", "bl"), None, None),
            P("chan"),
            P(None, ("chan", "bl")),
        ),
        out_specs=P("pol", None, "bl", "chan"),
        check_vma=False,
    )
```

```python
import functools
import math

import jax
import jax.numpy as jnp
import numpy as np
from jax import lax
from jax.experimental import pallas as pl
from jax.experimental.pallas import tpu as pltpu
from jax.sharding import PartitionSpec as P

G = 2048
SUB = 32
VB = 256
HALF = SUB // 2
LANES = 128
ROWS = 40
W_STEP = 0.25
f32 = jnp.float32
bf16 = jnp.bfloat16


def cos_sin(angle, terms):
    square = angle * angle
    cos_sum = f32((-1.0) ** (terms - 1) / math.factorial(2 * terms - 2))
    sin_sum = f32((-1.0) ** (terms - 1) / math.factorial(2 * terms - 1))
    for n in range(terms - 2, -1, -1):
        cos_sum = cos_sum * square + f32((-1.0) ** n / math.factorial(2 * n))
        sin_sum = sin_sum * square + f32((-1.0) ** n / math.factorial(2 * n + 1))
    return cos_sum, sin_sum * angle


def multiples(coords):
    c_half, s_half = cos_sin(coords * (math.pi / SUB), 6)
    cosines = {1: 1.0 - 2.0 * s_half * s_half}
    sines = {1: 2.0 * s_half * c_half}
    for k in range(2, HALF + 1):
        base = 1 << ((k - 1).bit_length() - 1)
        twice = 2.0 * cosines[base]
        if k == 2 * base:
            cosines[k] = twice * cosines[base] - 1.0
            sines[k] = twice * sines[base]
        else:
            cosines[k] = twice * cosines[k - base] - cosines[2 * base - k]
            sines[k] = twice * sines[k - base] + sines[2 * base - k]
    return cosines, sines


def odd_halves(coords):
    c_half, s_half = cos_sin(coords * (math.pi / SUB), 6)
    twice = {1: 2.0 - 4.0 * s_half * s_half}
    for base in (2, 4, 8):
        twice[base] = twice[base // 2] * twice[base // 2] - 2.0
    cosines, sines = [c_half], [s_half]
    for j in range(1, HALF):
        base = 1 << (j.bit_length() - 1)
        cosines.append(twice[base] * cosines[j - base] - cosines[2 * base - 1 - j])
        sines.append(twice[base] * sines[j - base] + sines[2 * base - 1 - j])
    return cosines, sines


GROUP = 8
BATCH = 10
PITCH = 11


def phases(start, scale, inputs, angles, values, wide):
    for group in range(BATCH):
        rows = pl.ds(pl.multiple_of((start + group * GROUP) * 4, 4 * GROUP), 4 * GROUP)
        for which, ref in enumerate(inputs):
            wide[which, : 4 * GROUP, :] = ref[rows, :].astype(f32)
        for part in range(2):
            at = (group * 2 + part) * PITCH * SUB

            def pick(which, component):
                return wide[which, pl.ds(part * 16 + component, 8, 2), :]

            def put(side, number, value):
                angles[side, at + number * PITCH : at + number * PITCH + 8, :] = value

            cosines, sines = multiples(pick(0, 0))
            for k in range(1, HALF + 1):
                put(0, k - 1, cosines[k])
                put(0, HALF + k - 1, sines[k])
            cosines, sines = odd_halves(pick(0, 1))
            for k in range(HALF):
                put(1, k, cosines[k])
                put(1, HALF + k, sines[k])
            c_half, s_half = cosines[0] * scale, sines[0] * scale
            chunks = slice((group * 2 + part) * 8, (group * 2 + part + 1) * 8)
            for product in range(2):
                real, imag = pick(1 + product, 0), pick(1 + product, 1)
                values[2 * product, chunks, :] = real * c_half + imag * s_half
                values[2 * product + 1, chunks, :] = imag * c_half - real * s_half


def add_products(id_at, ids_ref, angles, values, sums):
    ones = jnp.ones((HALF, VB), bf16)
    for block in range(BATCH * GROUP):
        lefts, rights = [], []
        for chunk in (2 * block, 2 * block + 1):
            at = pl.ds(chunk // 8 * PITCH * SUB + chunk % 8, SUB, PITCH)
            lefts.append(angles[0, at, :].astype(bf16))
            phase = angles[1, at, :]
            cosine, sine = phase[:HALF], phase[HALF:]
            pieces = []
            for product in range(2):
                real = values[2 * product, chunk : chunk + 1, :]
                imag = values[2 * product + 1, chunk : chunk + 1, :]
                rc, is_, rs, ic = real * cosine, imag * sine, real * sine, imag * cosine
                for piece in (rc - is_, rc + is_, ic + rs, ic - rs):
                    pieces.append(piece.astype(bf16))
            rights.append(jnp.concatenate(pieces, axis=0))
        image = lax.dot_general(
            jnp.concatenate([jnp.concatenate(lefts, axis=1), ones], axis=0),
            jnp.concatenate(rights, axis=1),
            (((1,), (1,)), ((), ())),
            preferred_element_type=f32,
        )
        at = pl.ds(pl.multiple_of(ids_ref[id_at + block] * ROWS, 8), ROWS)
        sums[at, :] += image[:ROWS]


def slot_sums_kernel(first_ref, sign_ref, ids_ref, uv_ref, mine_ref, theirs_ref, keep_ref, send_ref, sums, *scratch):
    local = (uv_ref, mine_ref, theirs_ref)
    blocks = uv_ref.shape[0] // 4
    step = BATCH * GROUP
    id_at = first_ref[0]
    scale = 0.5 / math.sqrt(VB)
    even, odd = scratch[:3], scratch[3:]
    sums[...] = jnp.zeros_like(sums)

    def fill(start, buffers):
        phases(start, scale, local, *buffers)

    def add(start, buffers):
        add_products(id_at + start, ids_ref, buffers[0], buffers[1], sums)

    fill(0, even)

    def two_batches(trip, carry):
        start = trip * 2 * step
        add(start, even)
        fill(start + step, odd)
        add(start + step, odd)
        fill(start + 2 * step, even)
        return carry

    trips = blocks // (2 * step) - 1
    lax.fori_loop(0, trips, two_batches, 0)
    add(trips * 2 * step, even)
    fill((trips * 2 + 1) * step, odd)
    add((trips * 2 + 1) * step, odd)

    owners = keep_ref.shape[0]
    pairs = sums.shape[0] // ROWS // owners // 2
    sign = sign_ref[0]
    low = lax.broadcasted_iota(jnp.int32, (1, LANES), 1) < LANES // 2

    def store(owner, rows, one, two):
        one_back, two_back = pltpu.roll(one, LANES // 2, 1), pltpu.roll(two, LANES // 2, 1)
        own = jnp.where(low, one_back + sign * one, two + sign * two_back)
        other = jnp.where(low, one - sign * one_back, two_back - sign * two)
        keep_ref[owner, rows, :] = own.astype(keep_ref.dtype)
        send_ref[owner, rows, :] = other.astype(send_ref.dtype)

    def store_owner(owner, carry):
        base = owner * (2 * pairs * ROWS)

        def rows_of(slot, row, count):
            return sums[pl.ds(pl.multiple_of(base + slot * ROWS + row, 8), count), :]

        for pair in range(pairs):
            store(
                owner, slice(pair * SUB, (pair + 1) * SUB), rows_of(pair, 0, SUB), rows_of(pairs + pair, 0, SUB)
            )
        blank = [jnp.zeros((16 - pairs, LANES), f32)]
        one = jnp.concatenate([rows_of(pair, SUB, 8)[:1] for pair in range(pairs)] + blank, axis=0)
        two = jnp.concatenate([rows_of(pairs + pair, SUB, 8)[:1] for pair in range(pairs)] + blank, axis=0)
        store(owner, slice(pairs * SUB, pairs * SUB + 16), one, two)
        return carry

    lax.fori_loop(0, owners, store_owner, 0)


def slot_sums(first, sign, block_slot, uv, mine, theirs, shard_count, slots):
    pairs = slots // 2
    rows = pairs * SUB + 16
    vmem = pl.BlockSpec(memory_space=pltpu.VMEM)
    smem = pl.BlockSpec(memory_space=pltpu.SMEM)
    buffers = [
        pltpu.VMEM((2, BATCH * 2 * PITCH * SUB + 16, LANES), f32),
        pltpu.VMEM((4, BATCH * 2 * GROUP, LANES), f32),
        pltpu.VMEM((3, 4 * GROUP + 8, LANES), f32),
    ]
    return pl.pallas_call(
        slot_sums_kernel,
        out_shape=[
            jax.ShapeDtypeStruct((shard_count, rows, LANES), f32),
            jax.ShapeDtypeStruct((shard_count, rows, LANES), bf16),
        ],
        in_specs=[smem, smem, smem, vmem, vmem, vmem],
        out_specs=[vmem, vmem],
        scratch_shapes=[pltpu.VMEM((shard_count * slots * ROWS, LANES), f32)]
        + buffers
        + buffers,
        compiler_params=pltpu.CompilerParams(vmem_limit_bytes=32 * 1024 * 1024),
        cost_estimate=pl.CostEstimate(flops=60_000_000_000, bytes_accessed=4_000_000, transcendentals=0),
        name="slot_sums",
    )(first, sign, block_slot, uv, mine, theirs)


def row_order():
    return np.array(list(range(HALF + 1, SUB)) + [HALF] + list(range(HALF - 1, -1, -1)))


def column_order():
    return np.array(list(range(HALF, SUB)) + list(range(HALF - 1, -1, -1)))


def dft_matrix():
    centred = np.arange(SUB) - HALF
    product_mod = centred[:, None] * centred[None, :] % SUB
    return np.exp(-2j * np.pi * product_mod / SUB) / math.sqrt(SUB)


def spread(matrix):
    parts = []
    for factor in (1, 1j):
        scaled = matrix * factor
        one = np.concatenate([scaled.real, scaled.imag], axis=1)
        parts.append(np.kron(np.eye(2), one))
    return np.concatenate(parts, axis=1).astype(np.float32)


def constants():
    rows_at, cols_at = row_order(), column_order()
    dft = dft_matrix()
    cols = dft.T[cols_at]
    columns = spread(np.concatenate([cols, 1j * cols], axis=0))
    rows = dft[:, rows_at]
    rows = np.concatenate([rows.real, rows.imag], axis=1).astype(np.float32)

    def outer(values):
        return values[rows_at][:, None], values[cols_at][None, :]

    place_x, place_y = outer((np.arange(SUB) - HALF) / SUB)
    taper_x, taper_y = outer(np.sin(np.pi * (np.arange(SUB) + 0.5) / SUB))
    n_term = np.sqrt(1.0 - place_x**2 - place_y**2) - 1.0
    turns = np.tile(-W_STEP * n_term, (1, 4)).astype(np.float32)
    tapers = np.tile(taper_x * taper_y, (1, 4)).astype(np.float32)

    def split(matrix):
        high = matrix.astype(jnp.bfloat16)
        return np.stack([high, (matrix - high.astype(np.float32)).astype(jnp.bfloat16)])

    return turns, tapers, split(columns), split(rows)


def halves(values):
    high = values.astype(bf16)
    return high, (values - high.astype(f32)).astype(bf16)


def dot_in_halves(left, right):
    (a, b), (c, d) = left, right
    small = jnp.dot(b, c, preferred_element_type=f32) + jnp.dot(a, d, preferred_element_type=f32)
    return small + jnp.dot(a, c, preferred_element_type=f32)


def transform_kernel(planes_ref, corners_ref, turns_ref, tapers_ref, columns_ref, rows_ref, *refs):
    sum_refs, out_ref = refs[:-1], refs[-1]
    pairs = out_ref.shape[0] // SUB
    plain = sum_refs[0][...].astype(f32)
    for sum_ref in sum_refs[1:]:
        plain = plain + sum_ref[...].astype(f32)
    lane = lax.broadcasted_iota(jnp.int32, (1, LANES), 1)
    turned = jnp.where(
        (lane // SUB) % 2 == 0, -pltpu.roll(plain, LANES - SUB, 1), pltpu.roll(plain, SUB, 1)
    )
    last = lax.broadcasted_iota(jnp.int32, (HALF, LANES), 0) == HALF - 1
    pieces = []
    for pair in range(pairs):
        at = pair * SUB
        cos_p, sin_p = plain[at : at + HALF], plain[at + HALF : at + SUB]
        cos_t, sin_t = turned[at : at + HALF], turned[at + HALF : at + SUB]
        zero = pairs * SUB + pair
        up = jnp.where(last, plain[zero : zero + 1], cos_p + sin_t)
        up_i = jnp.where(last, turned[zero : zero + 1], cos_t - sin_p)
        image = jnp.concatenate([up, cos_p - sin_t], axis=0)
        image_i = jnp.concatenate([up_i, cos_t + sin_p], axis=0)
        plane = jnp.where(lane < LANES // 2, planes_ref[pair], planes_ref[pairs + pair]).astype(f32)
        turns = plane * turns_ref[...]
        c_half, s_half = cos_sin((turns - jnp.floor(turns + 0.5)) * math.pi, 7)
        screen_cos = (1.0 - 2.0 * s_half * s_half) * tapers_ref[...]
        screen_sin = (2.0 * s_half * c_half) * tapers_ref[...]
        pieces.append(image * screen_cos + image_i * screen_sin)
    both = dot_in_halves(halves(jnp.concatenate(pieces, axis=0)), (columns_ref[0], columns_ref[1]))
    stacked = jnp.concatenate(
        [
            jnp.concatenate([both[pair * SUB : (pair + 1) * SUB, part : part + LANES] for pair in range(pairs)], axis=1)
            for part in (0, LANES)
        ],
        axis=0,
    )
    result = dot_in_halves((rows_ref[0], rows_ref[1]), halves(stacked)).astype(out_ref.dtype)
    for pair in range(pairs):
        out_ref[pair * SUB : (pair + 1) * SUB, :] = result[:, pair * LANES : (pair + 1) * LANES]
    out_ref[pairs * SUB :, :] = corners_ref[...].astype(out_ref.dtype)


def corner_rows(corners):
    digits = jnp.stack([corners // 16, corners % 16], axis=1).reshape(1, -1).astype(f32)
    return jnp.pad(digits, ((0, 15), (0, LANES - digits.shape[1])))


def subgrid_transform(sums, planes, corners, slots):
    vmem = pl.BlockSpec(memory_space=pltpu.VMEM)
    smem = pl.BlockSpec(memory_space=pltpu.SMEM)
    return pl.pallas_call(
        transform_kernel,
        out_shape=jax.ShapeDtypeStruct((slots // 2 * SUB + 16, LANES), bf16),
        in_specs=[smem] + [vmem] * (5 + len(sums)),
        out_specs=vmem,
        compiler_params=pltpu.CompilerParams(vmem_limit_bytes=32 * 1024 * 1024),
        name="subgrid_transform",
    )(planes, corner_rows(corners), *constants(), *sums)


def place_kernel(first, final, count, origin_ref, *refs):
    sub_refs = refs[:count]
    if final:
        out_ref, strip, decoded, corners, sem = refs[-5:]
    else:
        strip, decoded, corners, sem = refs[-4:]
    pairs = sub_refs[0].shape[0] // SUB
    slots = 2 * pairs
    for source, sub_ref in enumerate(sub_refs):
        digits = sub_ref[pairs * SUB :, :].astype(f32)
        joined = 16.0 * digits + pltpu.roll(digits, LANES - slots, 1)
        decoded[source * 8 : source * 8 + 8, :] = joined[:8].astype(jnp.int32)
    fetch = pltpu.make_async_copy(decoded, corners, sem.at[0, 0])
    fetch.start()
    if first:
        strip[...] = jnp.zeros_like(strip)
    lane = lax.broadcasted_iota(jnp.int32, (SUB, LANES), 1)
    cols = (strip.shape[1] - 2) * LANES
    fetch.wait()

    for source, sub_ref in enumerate(sub_refs):

        def add_pair(pair, carry, source=source, sub_ref=sub_ref):
            for half in range(2):
                row = corners[source * 8, half * pairs + pair] - origin_ref[0]
                col = corners[source * 8, 2 * slots + half * pairs + pair] - origin_ref[1]

                @pl.when((col > -SUB) & (col < cols))
                def _():
                    padded = col + LANES
                    tile = padded // LANES
                    at = padded % LANES
                    piece = sub_ref[pl.ds(pl.multiple_of(pair * SUB, SUB), SUB), :].astype(f32)
                    left = (lane >= at) & (lane < at + SUB)
                    right = lane < at + SUB - LANES
                    rows = pl.ds(row, SUB)
                    turned = [
                        pltpu.roll(piece, (at + (LANES - half * 2 * SUB - part * SUB)) % LANES, 1) for part in range(2)
                    ]
                    sums = [
                        strip[part, tile + over, rows, :] + jnp.where(mask, turned[part], 0.0)
                        for part in range(2)
                        for over, mask in enumerate((left, right))
                    ]
                    for part in range(2):
                        for over in range(2):
                            strip[part, tile + over, rows, :] = sums[2 * part + over]

            return carry

        lax.fori_loop(0, pairs, add_pair, 0)

    if final:
        copies = [
            pltpu.make_async_copy(
                strip.at[part, tile + 1, pl.ds(0, out_ref.shape[1]), :],
                out_ref.at[part, :, pl.ds(tile * LANES, LANES)],
                sem.at[part, tile],
            )
            for part in range(2)
            for tile in range(cols // LANES)
        ]
        for copy in copies:
            copy.start()
        for copy in copies:
            copy.wait()


def place(origin, subs, strip_rows, cols):
    smem = pl.BlockSpec(memory_space=pltpu.SMEM)
    vmem = pl.BlockSpec(memory_space=pltpu.VMEM)
    tiles = cols // LANES
    strip_shape = jax.ShapeDtypeStruct((2, tiles + 2, strip_rows + 8, LANES), f32)
    result = []
    for first, group in ((True, subs[:1] + subs[-1:]), (False, subs[1:-1])):
        outs, specs = [strip_shape], [vmem]
        if not first:
            outs = [jax.ShapeDtypeStruct((2, strip_rows, cols), f32)] + outs
            specs = [pl.BlockSpec(memory_space=pl.ANY)] + specs
        result = pl.pallas_call(
            functools.partial(place_kernel, first, not first, len(group)),
            out_shape=outs,
            in_specs=[smem] + [vmem] * (len(group) + len(result)),
            out_specs=specs,
            scratch_shapes=[
                pltpu.VMEM((8 * len(group), LANES), jnp.int32),
                pltpu.SMEM((8 * len(group), LANES), jnp.int32),
                pltpu.SemaphoreType.DMA((2, tiles)),
            ],
            input_output_aliases={} if first else {1 + len(group): 1},
            compiler_params=pltpu.CompilerParams(vmem_limit_bytes=32 * 1024 * 1024),
            name="place_own" if first else "place_others",
        )(origin, *group, *result)
    return result[0]


def around(block, axis):
    count = lax.axis_size(axis)
    return [block] + [
        lax.ppermute(block, axis, [(i, i ^ step) for i in range(count)]) for step in range(1, count)
    ]


def exchange(blocks, axis):
    count = lax.axis_size(axis)
    me = lax.axis_index(axis)

    def block_for(step):
        return lax.dynamic_index_in_dim(blocks, me ^ step, 0, keepdims=False)

    return [block_for(0)] + [
        lax.ppermute(block_for(step), axis, [(i, i ^ step) for i in range(count)])
        for step in range(1, count)
    ]


def on_device(visibilities, uv_coords, block_slot, slot_table):
    shard_count = lax.axis_size("bl")
    chan_count = lax.axis_size("chan")
    my_shard = lax.axis_index("bl")
    my_chan = lax.axis_index("chan")
    my_pol = lax.axis_index("pol")
    blocks = uv_coords.shape[0]
    slots = slot_table.shape[1]
    half = blocks // 2
    strip_rows = G // shard_count
    cols = G // chan_count

    def rows_of(values):
        count = values.shape[0]
        return values.reshape(count, 2, VB // LANES, LANES).transpose(0, 2, 1, 3).reshape(count * 4, LANES)

    vis = rows_of(visibilities[0])
    def half_of(rows, which):
        return lax.dynamic_slice_in_dim(rows, which * (half * 4), half * 4, 0)

    theirs = lax.ppermute(half_of(vis, 1 - my_pol), "pol", [(0, 1), (1, 0)])
    sign = (1.0 - 2.0 * my_pol.astype(f32))[None]
    first = (my_shard * blocks + my_pol * half)[None]
    coords, mine = lax.optimization_barrier((rows_of(uv_coords), vis))
    coords, mine = half_of(coords, my_pol), half_of(mine, my_pol)
    keep, send = slot_sums(first, sign, block_slot, coords, mine, theirs, shard_count, slots)
    got = lax.ppermute(send, "pol", [(0, 1), (1, 0)])
    partial = (keep + got.astype(f32)).astype(bf16)
    parts = exchange(partial, "bl")
    subs = around(subgrid_transform(parts, slot_table[2], slot_table[:2], slots), "chan")
    origin = jnp.stack([my_shard * strip_rows, my_chan * cols])
    return place(origin, subs, strip_rows, cols)[None]


def solution(mesh):
    return jax.shard_map(
        on_device,
        mesh=mesh,
        in_specs=(
            P("pol", ("chan", "bl"), None, None),
            P(("chan", "bl"), None, None),
            P("chan"),
            P(None, ("chan", "bl")),
        ),
        out_specs=P("pol", None, "bl", "chan"),
        check_vma=False,
    )
```
